128 devices in a mesh: ang: 8 (over z, x_hi), pos: 16 (over y, x_lo, core).
Axes of the slice: x: 4 (x_hi: 2, x_lo: 2; x = x_hi * 2 + x_lo), y: 4, z: 4, core: 2. Of those that a mesh axis runs over, the one named last changes fastest.
Arguments:
- object_init: float32 [16, 2, 512, 512], P('ang', None, 'pos'), may hold values from -4 to 4
- probe_field: float32 [2, 512, 512], replicated, may hold values from -4 to 4
- amplitudes: float32 [16, 16, 512, 512], P('ang', 'pos'), may hold values from 0.2 to 2
- offsets: int32 [16, 16, 2], P('ang', 'pos'), may hold values from 0 to 511
- slot_angle: int32 [16], replicated, may hold values from 0 to 15, each once
- conv_first: bfloat16 [3, 3, 32, 2], replicated, may hold values from -2 to 2
- bias_first: float32 [32], replicated, may hold values from -3 to 3
- conv_middle: bfloat16 [2, 3, 3, 32, 32], replicated, may hold values from -0.5 to 0.5
- bias_middle: float32 [2, 32], replicated, may hold values from -3 to 3
- conv_last: bfloat16 [3, 3, 32], replicated, may hold values from -0.5 to 0.5
Outputs:
- object_final: float32 [16, 2, 512, 512], P('ang', None, 'pos')
- projections: float32 [16, 8, 4, 16, 512], P('pos', 'ang')
The draws below stay inside these ranges and needn't reach their ends.
Inputs may be any that keep to these rules, and one draw needn't show every extreme that they name: `slot_angle`: each of the 16 angles is held by exactly one slot.
All inputs are finite; a program needn't handle non-finite values.
Results may differ from the reference program's by a relative error of at most 0.035.
Values may be sent and summed in bfloat16 or wider, within the bound.
A program may use at most 128 MiB of HBM per device.

```python
import math
import jax
import jax.numpy as jnp
from jax import lax

PIXELS = 512
ITERS = 2
CHANNELS = 32
MIDDLE = 2
ANGLES = 16
SHIFTS = 16
SLAB = 4
N_ANG = 8
N_POS = 16


def place_ends(drawn, key, low, largest):
    place = [jax.random.randint(jax.random.fold_in(key, axis), (), 0, length) for axis, length in enumerate(drawn.shape)]
    longest = drawn.shape.index(max(drawn.shape))
    next_to = place[:longest] + [(place[longest] + 1) % drawn.shape[longest]] + place[longest + 1:]
    return drawn.at[tuple(place)].set(low).at[tuple(next_to)].set(largest)


def block_levels(key, extent, split, low, top_value):
    def one(axis_at, blocks):
        heights = jax.random.uniform(jax.random.fold_in(jax.random.fold_in(key, 6), axis_at), (blocks,), jnp.float32, low / len(split), top_value / len(split))
        return jnp.repeat(jnp.exp(heights), extent[axis_at] // blocks).reshape((-1,) + (1,) * (len(extent) - axis_at - 1))

    loudness = one(*split[0])
    for cut in split[1:]:
        loudness = loudness * one(*cut)
    return loudness


def scatter_about(key, extent, deviation, reach, cuts=(), kind=jnp.bfloat16):
    array = deviation * jax.random.normal(key, extent, jnp.float32)
    if cuts:
        array = array * block_levels(key, extent, cuts, -0.22, 0.18)
    return jnp.clip(array, -reach, reach).astype(kind)


def setup_inputs(seed: int = 0) -> dict:
    seeds = jax.random.split(jax.random.key(seed), 11)
    return {
        "object_init": scatter_about(seeds[0], (ANGLES, 2, PIXELS, PIXELS), 0.7, 4.0, ((0, 8), (2, 16)), jnp.float32),
        "probe_field": scatter_about(seeds[1], (2, PIXELS, PIXELS), 0.7, 4.0, (), jnp.float32),
        "amplitudes": jnp.clip(jnp.exp(math.log(2.0) - 2.3025851 * jax.random.uniform(seeds[2], (ANGLES, SHIFTS, PIXELS, PIXELS), jnp.float32) ** block_levels(seeds[2], (ANGLES, SHIFTS, PIXELS, PIXELS), ((0, 8), (1, 16)), -0.2, 0.2)), 0.2, 2.0),
        "offsets": place_ends(jax.random.randint(seeds[3], (ANGLES, SHIFTS, 2), 0, PIXELS), jax.random.fold_in(seeds[3], 1), 0, PIXELS - 1).astype(jnp.int32),
        "slot_angle": jax.random.permutation(seeds[4], ANGLES).astype(jnp.int32),
        "conv_first": scatter_about(seeds[5], (3, 3, CHANNELS, 2), 9 ** -0.5, 2.0),
        "bias_first": scatter_about(seeds[6], (CHANNELS,), 0.5, 3.0, (), jnp.float32),
        "conv_middle": scatter_about(seeds[7], (MIDDLE, 3, 3, CHANNELS, CHANNELS), 144 ** -0.5, 0.5),
        "bias_middle": scatter_about(seeds[8], (MIDDLE, CHANNELS), 0.5, 3.0, (), jnp.float32),
        "conv_last": scatter_about(seeds[9], (3, 3, CHANNELS), 144 ** -0.5, 0.5),
    }


soften = 0.25
learning = 1.5

def make_tables(pixels):
    positions = jnp.arange(pixels, dtype=jnp.int32)
    frequency = jnp.where(positions < pixels // 2, positions, positions - pixels)
    product_mod = positions[:, None] * positions[None, :] % pixels
    chirp_turns = 3 * frequency * frequency % (8 * pixels)
    phase_turns = (8 * product_mod - chirp_turns[None, :]) % (8 * pixels)
    left_angle = phase_turns.astype(jnp.float32) * (2.0 * jnp.pi / (8 * pixels))
    right_angle = product_mod.astype(jnp.float32) * (2.0 * jnp.pi / pixels)
    left_real = jnp.cos(left_angle)
    left_imag = jnp.sin(left_angle)
    right_real = jnp.cos(right_angle)
    right_imag = -jnp.sin(right_angle)
    highest = lax.Precision.HIGHEST
    mat_real = (jnp.dot(left_real, right_real, precision=highest) - jnp.dot(left_imag, right_imag, precision=highest)) / pixels
    mat_imag = (jnp.dot(left_real, right_imag, precision=highest) + jnp.dot(left_imag, right_real, precision=highest)) / pixels
    mat_real = mat_real.astype(jnp.bfloat16)
    mat_imag = mat_imag.astype(jnp.bfloat16)
    forward_block = jnp.concatenate([jnp.concatenate([mat_real, -mat_imag], 1), jnp.concatenate([mat_imag, mat_real], 1)], 0)
    backward_block = jnp.concatenate([jnp.concatenate([mat_real, mat_imag], 1), jnp.concatenate([-mat_imag, mat_real], 1)], 0)
    row_matrix = jnp.concatenate([mat_real, mat_imag], 1)
    return (forward_block, backward_block, row_matrix)

def left_apply(block, field_pair):
    pixels = field_pair.shape[1]
    result = jnp.dot(block, field_pair.reshape(2 * pixels, pixels), preferred_element_type=jnp.float32)
    return result.reshape(2, pixels, pixels)

def right_apply(near_pair, row_matrix, conjugate):
    pixels = near_pair.shape[1]
    product = jnp.dot(near_pair.reshape(2 * pixels, pixels), row_matrix, preferred_element_type=jnp.float32)
    real_real = product[:pixels, :pixels]
    real_imag = product[:pixels, pixels:]
    imag_real = product[pixels:, :pixels]
    imag_imag = product[pixels:, pixels:]
    if conjugate:
        return jnp.stack([real_real + imag_imag, imag_real - real_imag])
    return jnp.stack([real_real - imag_imag, real_imag + imag_real])

def field_term(view_pair, probe_field, amplitude, row_shift, col_shift, tables):
    forward_block, backward_block, row_matrix = tables
    moved = jnp.roll(view_pair, (row_shift, col_shift), axis=(1, 2))
    probe_real = probe_field[0]
    probe_imag = probe_field[1]
    exit_real = probe_real * moved[0] - probe_imag * moved[1]
    exit_imag = probe_real * moved[1] + probe_imag * moved[0]
    exit_wave = jnp.stack([exit_real, exit_imag]).astype(jnp.bfloat16)
    near_wave = left_apply(forward_block, exit_wave).astype(jnp.bfloat16)
    wave = right_apply(near_wave, row_matrix, False)
    magnitude = jnp.sqrt(wave[0] * wave[0] + wave[1] * wave[1] + soften)
    misfit = (wave * (1.0 - amplitude / magnitude)[None]).astype(jnp.bfloat16)
    back_near = left_apply(backward_block, misfit).astype(jnp.bfloat16)
    back_wave = right_apply(back_near, row_matrix, True)
    term_real = probe_real * back_wave[0] + probe_imag * back_wave[1]
    term_imag = probe_real * back_wave[1] - probe_imag * back_wave[0]
    return jnp.roll(jnp.stack([term_real, term_imag]), (-row_shift, -col_shift), axis=(1, 2))

def shift_along(values, offset, axis):
    if offset == 0:
        return values
    length = values.shape[axis]
    padding = jnp.zeros_like(lax.slice_in_dim(values, 0, 1, axis=axis))
    if offset > 0:
        return jnp.concatenate([lax.slice_in_dim(values, 1, length, axis=axis), padding], axis)
    return jnp.concatenate([padding, lax.slice_in_dim(values, 0, length - 1, axis=axis)], axis)

def conv_layer(inputs, weights):
    running = None
    for row_tap in range(3):
        along_angle = shift_along(inputs, row_tap - 1, 2)
        stacked = jnp.concatenate([shift_along(along_angle, col_tap - 1, 3) for col_tap in range(3)], 0)
        merged = jnp.concatenate([weights[row_tap, col_tap] for col_tap in range(3)], 1)
        piece_sum = jnp.einsum('oc,csaw->osaw', merged, stacked, preferred_element_type=jnp.float32)
        running = piece_sum if running is None else running + piece_sum
    return running

def network(inputs, conv_first, bias_first, conv_middle, bias_middle, conv_last):
    hidden = jax.nn.relu(conv_layer(inputs, conv_first) + bias_first[:, None, None, None]).astype(jnp.bfloat16)
    for layer_index in range(conv_middle.shape[0]):
        raised = conv_layer(hidden, conv_middle[layer_index]) + bias_middle[layer_index][:, None, None, None]
        hidden = jax.nn.relu(raised).astype(jnp.bfloat16)
    return conv_layer(hidden, conv_last[:, :, None, :])[0]

def reorder_angles(height_slabs, slot_angle):
    count = height_slabs.shape[0]
    selector = (slot_angle[None, :] == jnp.arange(count, dtype=jnp.int32)[:, None]).astype(jnp.bfloat16)
    return jnp.einsum('kj,jcsw->cskw', selector, height_slabs, preferred_element_type=jnp.float32).astype(jnp.bfloat16)

def reference(object_init, probe_field, amplitudes, offsets, slot_angle, conv_first, bias_first, conv_middle, bias_middle, conv_last):
    pixels = object_init.shape[2]
    tables = make_tables(pixels)
    step_size = learning / SHIFTS
    current = object_init
    for sweep_index in range(ITERS):

        def per_angle(angle_item):
            object_angle, amp_angle, offset_angle = angle_item
            view_pair = object_angle.astype(jnp.bfloat16)

            def per_shift(running, shift_item):
                amp_one, offset_one = shift_item
                added = field_term(view_pair, probe_field, amp_one, offset_one[0], offset_one[1], tables)
                return (running + added, None)
            running, unused = lax.scan(per_shift, jnp.zeros(object_angle.shape, jnp.float32), (amp_angle, offset_angle))
            return running
        gradient = lax.map(per_angle, (current, amplitudes, offsets))
        current = current - step_size * gradient
    sinogram = reorder_angles(current.astype(jnp.bfloat16), slot_angle)
    blocks = sinogram.reshape(2, pixels // SLAB, SLAB, ANGLES, pixels)
    blocks = jnp.moveaxis(blocks, 1, 0)

    def per_block(block):
        return network(block, conv_first, bias_first, conv_middle, bias_middle, conv_last)
    outputs = lax.map(per_block, blocks)
    projections = outputs.reshape(N_POS, N_ANG, SLAB, ANGLES, pixels)
    return (current, projections)
```

```python
import functools

import jax
import jax.numpy as jnp
import ml_dtypes
import numpy as np
from jax import lax
from jax.experimental import pallas as pl
from jax.experimental.pallas import tpu as pltpu
from jax.sharding import PartitionSpec as P

soften = 0.25
learning = 1.5
N = 512
B = 128
f32 = jnp.float32
bf16 = jnp.bfloat16
MESH = pl.DeviceIdType.MESH


def make_tables():
    f = np.arange(N)
    g = np.where(f < N // 2, f, f - N).astype(np.float64)
    lam = np.exp(-3j * np.pi * g * g / (4 * N))
    d = np.arange(B)[:, None] - np.arange(B)[None, :]
    blocks = []
    for m in range(4):
        fm = np.arange(m, N, 4)
        c = (lam[fm] * np.exp(2j * np.pi * fm * d[:, :, None] / N)).sum(-1) / N
        blocks.append(np.block([[c.real, -c.imag], [c.imag, c.real]]))
    left = np.stack(blocks)
    turned = np.ascontiguousarray(np.swapaxes(left, 1, 2))
    return left.astype(ml_dtypes.bfloat16), turned.astype(ml_dtypes.bfloat16)


def add(a, b):
    return (a[0] + b[0], a[1] + b[1])


def sub(a, b):
    return (a[0] - b[0], a[1] - b[1])


def add_i(a, b):
    return (a[0] - b[1], a[1] + b[0])


def sub_i(a, b):
    return (a[0] + b[1], a[1] - b[0])


def fold(x):
    t0, t1, t2, t3 = add(x[0], x[2]), sub(x[0], x[2]), add(x[1], x[3]), sub(x[1], x[3])
    return [add(t0, t2), sub_i(t1, t3), sub(t0, t2), add_i(t1, t3)]


def unfold(x):
    t0, t1, t2, t3 = add(x[0], x[2]), sub(x[0], x[2]), add(x[1], x[3]), sub(x[1], x[3])
    return [add(t0, t2), add_i(t1, t3), sub(t0, t2), sub_i(t1, t3)]


def fold2(e):
    rows = [fold(e[q]) for q in range(4)]
    cols = [fold([rows[q][m] for q in range(4)]) for m in range(4)]
    return [[cols[mc][mr] for mc in range(4)] for mr in range(4)]


def unfold2(e):
    cols = [unfold([e[q][m] for q in range(4)]) for m in range(4)]
    return [unfold([cols[m][q] for m in range(4)]) for q in range(4)]


def lanes(q):
    return slice(q * B, q * B + B)


def store_y(ya, y, row, n):
    for mr in range(4):
        for mc in range(4):
            for ri in range(2):
                ya[pl.ds((mr * 2 + ri) * B + row, n), lanes(mc)] = y[mr][mc][ri].astype(bf16)


def load_f(f, row, n):
    return [
        [
            tuple(f[pl.ds((mr * 2 + ri) * B + row, n), lanes(mc)] for ri in range(2))
            for mc in range(4)
        ]
        for mr in range(4)
    ]


ROWS = 16


def stage1(v, pr, ya):
    n = ROWS

    def body(g, _):
        row = pl.multiple_of(g * n, n)
        tile = g * n // 32
        part = pl.multiple_of(lax.rem(g * n, 32), n)
        e = []
        for q in range(4):
            line = []
            for c in range(4):
                vr = v[q * 4 + tile, 0, pl.ds(part, n), lanes(c)].astype(f32)
                vi = v[q * 4 + tile, 1, pl.ds(part, n), lanes(c)].astype(f32)
                a = pr[0, pl.ds(q * B + row, n), lanes(c)].astype(f32)
                b = pr[1, pl.ds(q * B + row, n), lanes(c)].astype(f32)
                line.append((a * vr - b * vi, a * vi + b * vr))
            e.append(line)
        store_y(ya, fold2(e), row, n)
        return 0

    lax.fori_loop(0, B // n, body, 0)


def right(ya, mats, out, dtype):
    for mc in range(4):
        lhs = jnp.concatenate(
            [
                jnp.concatenate(
                    [
                        ya[(mr * 2 + ri) * B : (mr * 2 + ri + 1) * B, lanes(mc)]
                        for ri in range(2)
                    ],
                    1,
                )
                for mr in range(4)
            ],
            0,
        )
        r = jnp.dot(lhs, mats[mc], preferred_element_type=f32)
        for mr in range(4):
            for ri in range(2):
                out[(mr * 2 + ri) * B : (mr * 2 + ri + 1) * B, lanes(mc)] = r[
                    mr * B : mr * B + B, lanes(ri)
                ].astype(dtype)


def left(mats, yb, out, dtype):
    for mr in range(4):
        out[mr * 256 : mr * 256 + 256, :] = jnp.dot(
            mats[mr], yb[mr * 256 : mr * 256 + 256, :], preferred_element_type=f32
        ).astype(dtype)


def stage2(f, am, ya):
    n = ROWS

    def body(g, _):
        row = pl.multiple_of(g * n, n)
        w = unfold2(load_f(f, row, n))
        for q in range(4):
            for c in range(4):
                wr, wi = w[q][c]
                a = am[pl.ds(q * B + row, n), lanes(c)].astype(f32)
                s = 1.0 - a * lax.rsqrt(wr * wr + wi * wi + soften)
                w[q][c] = (wr * s, wi * s)
        store_y(ya, fold2(w), row, n)
        return 0

    lax.fori_loop(0, B // n, body, 0)


def stage3(f, pr, g, x, cls):
    n = ROWS

    def body(k, _):
        part = pl.multiple_of(k * n, n)
        row = pl.multiple_of((2 * x + cls) * 32 + k * n, n)
        tot = None
        for i in range(2):
            w = unfold2(load_f(f.at[i], row, n))
            new = []
            for q in range(4):
                for c in range(4):
                    a = pr[i, 0, pl.ds(q * B + row, n), lanes(c)].astype(f32)
                    b = pr[i, 1, pl.ds(q * B + row, n), lanes(c)].astype(f32)
                    br, bi = w[q][c]
                    new.append((a * br + b * bi, a * bi - b * br))
            tot = new if tot is None else [add(p, q) for p, q in zip(tot, new)]
        for q in range(4):
            for c in range(4):
                for ri in range(2):
                    g[q, ri, pl.ds(part, n), lanes(c)] = tot[q * 4 + c][ri].astype(g.dtype)
        return 0

    lax.fori_loop(0, 32 // n, body, 0)


def one_hot(offset, transpose):
    a = lax.broadcasted_iota(jnp.int32, (N, N), 0)
    b = lax.broadcasted_iota(jnp.int32, (N, N), 1)
    if transpose:
        return jnp.where(a == ((b + offset) & (N - 1)), 1.0, 0.0).astype(bf16)
    return jnp.where(b == ((a + offset) & (N - 1)), 1.0, 0.0).astype(bf16)


def make_hot(off, hot):
    hot[0] = one_hot(off[0:1, 0:1], False)
    hot[1] = one_hot(off[8:9, 0:1], True)


def roll_plane(src, hot, tmp, dst):
    for h in range(2):
        sl = slice(h * 256, h * 256 + 256)
        tmp[sl, :] = jnp.dot(hot[0, sl, :], src[...], preferred_element_type=f32).astype(bf16)
    for h in range(2):
        sl = slice(h * 256, h * 256 + 256)
        dst[sl, :] = jnp.dot(tmp[sl, :], hot[1], preferred_element_type=f32).astype(bf16)


def main_kernel(
    obj,
    probe_hbm,
    amps_hbm,
    off,
    mat_l,
    mat_r,
    obj_out,
    nb_out,
    view,
    probe_in,
    amps_in,
    probe16,
    amp16,
    amp_send,
    amp_recv,
    off_own,
    off_send,
    off_recv,
    hot,
    tmp,
    pr,
    am,
    ya,
    yb,
    ff,
    x_obj,
    g_send,
    g_recv,
    g_own,
    sa,
    sb,
    ra,
    rb,
    total,
    xg_send,
    xg_recv,
    as_send,
    nb,
    local_sem,
    x_sem,
    ag_recv,
    ring_send,
    sib_send,
    gs_sem,
    gr_sem,
    sa_sem,
    sb_sem,
    ra_sem,
    rb_sem,
    aa_send,
    aa_recv,
):
    pos = lax.axis_index("pos")
    ang = lax.axis_index("ang")
    c = lax.rem(pos, 2)
    s = lax.rem(pos // 2, 2)
    y = pos // 4
    up = lax.rem(y + 1, 4)
    down = lax.rem(y + 3, 4)
    far = lax.rem(y + 2, 4)

    def at(yy, xx, cc):
        return yy * 4 + xx * 2 + cc

    dev_up = (ang, at(up, s, c))
    dev_down = (ang, at(down, s, c))
    dev_x = (ang, at(y, 1 - s, c))
    dev_sib = (ang, at(y, s, 1 - c))
    step_size = learning / 16

    def rc(src, dst, send, recv, dev):
        return pltpu.make_async_remote_copy(
            src_ref=src, dst_ref=dst, send_sem=send, recv_sem=recv, device_id=dev,
            device_id_type=MESH,
        )

    def arrived(dst, recv):
        rc(dst, dst, recv, recv, dev_x).wait_recv()

    def left_dev(src, send):
        rc(src, src, send, send, dev_x).wait_send()

    cp_probe = pltpu.make_async_copy(probe_hbm, probe_in, local_sem.at[0])
    cp_amps = pltpu.make_async_copy(amps_hbm, amps_in, local_sem.at[1])
    cp_amps.start()
    cp_probe.start()

    barrier = pltpu.get_barrier_semaphore()
    for dev in (dev_up, dev_down, dev_x, dev_sib):
        pl.semaphore_signal(barrier, inc=1, device_id=dev, device_id_type=MESH)
    for d in range(1, 8):
        pl.semaphore_signal(
            barrier, inc=1, device_id=(lax.rem(ang + d, 8), pos), device_id_type=MESH
        )

    own = at(y, s, c)
    other = at(y, 1 - s, c)
    view[0, own] = obj[s].astype(bf16)
    x_obj[...] = obj[1 - s].astype(bf16)
    for i, (ref, slot) in enumerate(((off_own, s), (off_send, 1 - s))):
        for k in range(2):
            value = jnp.where(slot == 0, off[0, 0, k], off[1, 0, k])
            ref[k * 8 : k * 8 + 8, :] = jnp.full((8, 128), value, jnp.int32)

    pl.semaphore_wait(barrier, 11)

    rc(x_obj, view.at[0, own], x_sem.at[0], ag_recv.at[0, own], dev_x).start()
    rc(off_send, off_recv, x_sem.at[1], x_sem.at[2], dev_x).start()

    def ag_start(k, xx):
        tile = at(y, xx, c)
        ref = view.at[k, tile]
        rc(ref, ref, ring_send.at[k, xx, 0], ag_recv.at[k, tile], dev_up).start()
        rc(ref, ref, ring_send.at[k, xx, 1], ag_recv.at[k, tile], dev_down).start()
        rc(ref, ref, sib_send.at[k, 0, xx], ag_recv.at[k, tile], dev_sib).start()

    def ag_take(k, yy, xx, rel, forward):
        tile = at(yy, xx, c)
        ref = view.at[k, tile]
        arrived(ref, ag_recv.at[k, tile])
        if forward is not None:
            rc(ref, ref, ring_send.at[k, 2, forward], ag_recv.at[k, tile],
               dev_up if forward == 0 else dev_down).start()
        rc(ref, ref, sib_send.at[k, rel, xx], ag_recv.at[k, tile], dev_sib).start()

    def ag_relay(k):
        ag_take(k, down, 0, 1, 0)
        ag_take(k, up, 1, 2, 1)

    def ag_finish(k):
        ag_take(k, down, 1, 1, None)
        ag_take(k, up, 0, 2, None)
        ag_take(k, far, 0, 3, None)
        ag_take(k, far, 1, 3, None)
        for yy in range(4):
            for xx in range(2):
                tile = at(yy, xx, 1 - c)
                arrived(view.at[k, tile], ag_recv.at[k, tile])

    def ag_sent(k):
        for xx in range(2):
            tile = at(y, xx, c)
            for d in range(2):
                left_dev(view.at[k, tile], ring_send.at[k, xx, d])
        left_dev(view.at[k, at(down, 0, c)], ring_send.at[k, 2, 0])
        left_dev(view.at[k, at(up, 1, c)], ring_send.at[k, 2, 1])
        for rel, yy in enumerate((y, down, up, far)):
            for xx in range(2):
                left_dev(view.at[k, at(yy, xx, c)], sib_send.at[k, rel, xx])

    ag_start(0, s)
    cp_amps.wait()
    amp_send[...] = amps_in[1 - s, 0].astype(bf16)
    cp_amp_x = rc(amp_send, amp_recv, x_sem.at[3], x_sem.at[4], dev_x)
    cp_amp_x.start()
    amp16[...] = amps_in[s, 0].astype(bf16)
    arrived(view.at[0, other], ag_recv.at[0, other])
    ag_start(0, 1 - s)
    cp_probe.wait()
    probe16[...] = probe_in[...].astype(bf16)
    make_hot(off_own, hot.at[0])
    roll_plane(probe16.at[0], hot.at[0], tmp, pr.at[0, 0])
    roll_plane(probe16.at[1], hot.at[0], tmp, pr.at[0, 1])
    ag_relay(0)
    roll_plane(amp16, hot.at[0], tmp, am.at[0])
    arrived(off_recv, x_sem.at[2])
    make_hot(off_recv, hot.at[1])
    roll_plane(probe16.at[0], hot.at[1], tmp, pr.at[1, 0])
    roll_plane(probe16.at[1], hot.at[1], tmp, pr.at[1, 1])

    for k in range(2):
        if k == 1:
            ag_relay(k)
        ag_finish(k)
        for i in range(2):
            stage1(view.at[k], pr.at[i], ya.at[i])
            right(ya.at[i], mat_r, yb.at[i], bf16)
            left(mat_l, yb.at[i], ff.at[i], f32)
        if k == 0:
            arrived(amp_recv, x_sem.at[4])
            roll_plane(amp_recv, hot.at[1], tmp, am.at[1])
        for i in range(2):
            stage2(ff.at[i], am.at[i], ya.at[i])
            left(mat_r, ya.at[i], yb.at[i], bf16)
            right(yb.at[i], mat_l, ff.at[i], f32)
        for xx in range(2):
            stage3(ff, pr, g_send.at[k, xx], xx, 1 - c)
            rc(g_send.at[k, xx], g_recv.at[k, xx], gs_sem.at[k, xx], gr_sem.at[k, xx],
               dev_sib).start()
        for xx in range(2):
            stage3(ff, pr, g_own.at[xx], xx, c)
        ag_sent(k)

        def comb(yy, xx):
            return g_own[xx, yy] + g_recv[k, xx, yy].astype(f32)

        def push(buf, sem, dst, dsem, j, value, dev):
            buf[k, j] = value.astype(bf16)
            rc(buf.at[k, j], dst.at[k, j], sem.at[k, j], dsem.at[k, j], dev).start()

        arrived(g_recv.at[k, 0], gr_sem.at[k, 0])
        push(sa, sa_sem, ra, ra_sem, 0, comb(far, 0), dev_up)
        arrived(g_recv.at[k, 1], gr_sem.at[k, 1])
        push(sb, sb_sem, rb, rb_sem, 0, comb(far, 1), dev_down)
        push(sa, sa_sem, ra, ra_sem, 2, comb(up, 1), dev_up)
        push(sb, sb_sem, rb, rb_sem, 2, comb(down, 0), dev_down)
        arrived(ra.at[k, 0], ra_sem.at[k, 0])
        push(sa, sa_sem, ra, ra_sem, 1, comb(up, 0) + ra[k, 0].astype(f32), dev_up)
        arrived(rb.at[k, 0], rb_sem.at[k, 0])
        push(sb, sb_sem, rb, rb_sem, 1, comb(down, 1) + rb[k, 0].astype(f32), dev_down)
        for j in (2, 1):
            arrived(ra.at[k, j], ra_sem.at[k, j])
            arrived(rb.at[k, j], rb_sem.at[k, j])
        t0 = comb(y, 0) + ra[k, 1].astype(f32) + rb[k, 2].astype(f32)
        t1 = comb(y, 1) + ra[k, 2].astype(f32) + rb[k, 1].astype(f32)
        if k == 0:
            total[0] = t0
            total[1] = t1
            view[1, own] = (obj[s] - step_size * total[s]).astype(bf16)
            view[1, other] = (
                view[0, other].astype(f32) - step_size * total[1 - s]
            ).astype(bf16)
            ag_start(1, 0)
            ag_start(1, 1)
        else:
            total[0] = total[0] + t0
            total[1] = total[1] + t1
        for j in range(3):
            left_dev(sa.at[k, j], sa_sem.at[k, j])
            left_dev(sb.at[k, j], sb_sem.at[k, j])
        for xx in range(2):
            left_dev(g_send.at[k, xx], gs_sem.at[k, xx])

    xg_send[...] = total[1 - s].astype(bf16)
    cp_xg = rc(xg_send, xg_recv, x_sem.at[5], x_sem.at[6], dev_x)
    cp_xg.start()
    obj_out[s] = obj[s] - step_size * total[s]
    cp_xg.wait_recv()
    obj_out[1 - s] = obj[1 - s] - step_size * xg_recv[...].astype(f32)
    for g in range(8):
        as_send[g] = jnp.concatenate(
            [obj_out[sl, ri, g * 4 : g * 4 + 4, :] for sl in range(2) for ri in range(2)], 0
        ).astype(bf16)

    def a2a(d):
        to = lax.rem(ang + d, 8)
        return rc(as_send.at[to], nb.at[ang], aa_send.at[d], aa_recv.at[ang], (to, pos))

    for d in range(1, 8):
        a2a(d).start()
    nb[ang] = as_send[ang]
    for d in range(1, 8):
        frm = lax.rem(ang + d, 8)
        arrived(nb.at[frm], aa_recv.at[frm])
    nb_out[...] = nb[...]
    for d in range(1, 8):
        a2a(d).wait_send()
    cp_xg.wait_send()
    left_dev(x_obj, x_sem.at[0])
    left_dev(off_send, x_sem.at[1])
    cp_amp_x.wait_send()


def sweeps(object_init, probe_field, amplitudes, offsets):
    mat_l, mat_r = make_tables()
    vm = pl.BlockSpec(memory_space=pltpu.VMEM)
    hbm = pl.BlockSpec(memory_space=pl.ANY)
    tile = (2, 32, N)
    scratch = [
        pltpu.VMEM((2, 16) + tile, bf16),
        pltpu.VMEM((2, N, N), f32),
        pltpu.VMEM((2, 1, N, N), f32),
        pltpu.VMEM((2, N, N), bf16),
        pltpu.VMEM((N, N), bf16),
        pltpu.VMEM((N, N), bf16),
        pltpu.VMEM((N, N), bf16),
        pltpu.VMEM((16, 128), jnp.int32),
        pltpu.VMEM((16, 128), jnp.int32),
        pltpu.VMEM((16, 128), jnp.int32),
        pltpu.VMEM((2, 2, N, N), bf16),
        pltpu.VMEM((N, N), bf16),
        pltpu.VMEM((2, 2, N, N), bf16),
        pltpu.VMEM((2, N, N), bf16),
        pltpu.VMEM((2, 2 * N, N), bf16),
        pltpu.VMEM((2, 2 * N, N), bf16),
        pltpu.VMEM((2, 2 * N, N), f32),
        pltpu.VMEM(tile, bf16),
        pltpu.VMEM((2, 2, 4) + tile, bf16),
        pltpu.VMEM((2, 2, 4) + tile, bf16),
        pltpu.VMEM((2, 4) + tile, f32),
        pltpu.VMEM((2, 3) + tile, bf16),
        pltpu.VMEM((2, 3) + tile, bf16),
        pltpu.VMEM((2, 3) + tile, bf16),
        pltpu.VMEM((2, 3) + tile, bf16),
        pltpu.VMEM((2,) + tile, f32),
        pltpu.VMEM(tile, bf16),
        pltpu.VMEM(tile, bf16),
        pltpu.VMEM((8, 16, N), bf16),
        pltpu.VMEM((8, 16, N), bf16),
        pltpu.SemaphoreType.DMA((2,)),
        pltpu.SemaphoreType.DMA((7,)),
        pltpu.SemaphoreType.DMA((2, 16)),
        pltpu.SemaphoreType.DMA((2, 3, 2)),
        pltpu.SemaphoreType.DMA((2, 4, 2)),
        pltpu.SemaphoreType.DMA((2, 2)),
        pltpu.SemaphoreType.DMA((2, 2)),
        pltpu.SemaphoreType.DMA((2, 3)),
        pltpu.SemaphoreType.DMA((2, 3)),
        pltpu.SemaphoreType.DMA((2, 3)),
        pltpu.SemaphoreType.DMA((2, 3)),
        pltpu.SemaphoreType.DMA((8,)),
        pltpu.SemaphoreType.DMA((8,)),
    ]
    return pl.pallas_call(
        main_kernel,
        out_shape=(
            jax.ShapeDtypeStruct((2,) + tile, f32),
            jax.ShapeDtypeStruct((8, 16, N), bf16),
        ),
        in_specs=[vm, hbm, hbm, pl.BlockSpec(memory_space=pltpu.SMEM), vm, vm],
        out_specs=(vm, vm),
        scratch_shapes=scratch,
        compiler_params=pltpu.CompilerParams(
            collective_id=0, has_side_effects=True, vmem_limit_bytes=48 << 20
        ),
        cost_estimate=pl.CostEstimate(
            flops=12_000_000_000, bytes_accessed=8_000_000, transcendentals=1_000_000
        ),
    )(object_init, probe_field, amplitudes, offsets, jnp.asarray(mat_l), jnp.asarray(mat_r))


def shift_along(values, offset, axis):
    if offset == 0:
        return values
    length = values.shape[axis]
    padding = jnp.zeros_like(lax.slice_in_dim(values, 0, 1, axis=axis))
    if offset > 0:
        return jnp.concatenate([lax.slice_in_dim(values, 1, length, axis=axis), padding], axis)
    return jnp.concatenate([padding, lax.slice_in_dim(values, 0, length - 1, axis=axis)], axis)


def conv_layer(inputs, weights):
    running = None
    for row_tap in range(3):
        along_angle = shift_along(inputs, row_tap - 1, 2)
        stacked = jnp.concatenate(
            [shift_along(along_angle, col_tap - 1, 3) for col_tap in range(3)], 0
        )
        merged = jnp.concatenate([weights[row_tap, col_tap] for col_tap in range(3)], 1)
        piece_sum = jnp.einsum("oc,csaw->osaw", merged, stacked, preferred_element_type=jnp.float32)
        running = piece_sum if running is None else running + piece_sum
    return running


def network(inputs, conv_first, bias_first, conv_middle, bias_middle, conv_last):
    hidden = jax.nn.relu(conv_layer(inputs, conv_first) + bias_first[:, None, None, None]).astype(
        jnp.bfloat16
    )
    for layer_index in range(conv_middle.shape[0]):
        raised = (
            conv_layer(hidden, conv_middle[layer_index])
            + bias_middle[layer_index][:, None, None, None]
        )
        hidden = jax.nn.relu(raised).astype(jnp.bfloat16)
    return conv_layer(hidden, conv_last[:, :, None, :])[0]


def reorder_angles(height_slabs, slot_angle):
    count = height_slabs.shape[0]
    selector = (slot_angle[None, :] == jnp.arange(count, dtype=jnp.int32)[:, None]).astype(
        jnp.bfloat16
    )
    return jnp.einsum(
        "kj,jcsw->cskw", selector, height_slabs, preferred_element_type=jnp.float32
    ).astype(jnp.bfloat16)


def on_device(
    object_init,
    probe_field,
    amplitudes,
    offsets,
    slot_angle,
    conv_first,
    bias_first,
    conv_middle,
    bias_middle,
    conv_last,
):
    object_tile, slabs = sweeps(object_init, probe_field, amplitudes, offsets)
    ordered = reorder_angles(slabs.reshape(16, 2, 4, N), slot_angle)
    outputs = network(ordered, conv_first, bias_first, conv_middle, bias_middle, conv_last)
    return (object_tile, outputs[None, None])


def solution(mesh):
    return jax.shard_map(
        on_device,
        mesh=mesh,
        in_specs=(
            P("ang", None, "pos", None),
            P(),
            P("ang", "pos", None, None),
            P("ang", "pos", None),
            P(),
            P(),
            P(),
            P(),
            P(),
            P(),
        ),
        out_specs=(P("ang", None, "pos", None), P("pos", "ang", None, None, None)),
        check_vma=False,
    )
```

```python
import functools

import jax
import jax.numpy as jnp
import ml_dtypes
import numpy as np
from jax import lax
from jax.experimental import pallas as pl
from jax.experimental.pallas import tpu as pltpu
from jax.sharding import PartitionSpec as P

soften = 0.25
learning = 1.5
N = 512
B = 128
f32 = jnp.float32
bf16 = jnp.bfloat16
MESH = pl.DeviceIdType.MESH


def make_tables():
    f = np.arange(N)
    g = np.where(f < N // 2, f, f - N).astype(np.float64)
    lam = np.exp(-3j * np.pi * g * g / (4 * N))
    d = np.arange(B)[:, None] - np.arange(B)[None, :]
    blocks = []
    for m in range(4):
        fm = np.arange(m, N, 4)
        c = (lam[fm] * np.exp(2j * np.pi * fm * d[:, :, None] / N)).sum(-1) / N
        blocks.append(np.block([[c.real, -c.imag], [c.imag, c.real]]))
    left = np.stack(blocks)
    pair = np.stack([left, np.swapaxes(left, 1, 2)]).astype(ml_dtypes.bfloat16)
    orders = [np.arange(256) ^ (32 * k) for k in range(4)]
    return np.stack([pair[:, :, order][:, :, :, order] for order in orders])


def add(a, b):
    return (a[0] + b[0], a[1] + b[1])


def sub(a, b):
    return (a[0] - b[0], a[1] - b[1])


def add_i(a, b):
    return (a[0] - b[1], a[1] + b[0])


def sub_i(a, b):
    return (a[0] + b[1], a[1] - b[0])


def fold(x):
    t0, t1, t2, t3 = add(x[0], x[2]), sub(x[0], x[2]), add(x[1], x[3]), sub(x[1], x[3])
    return [add(t0, t2), sub_i(t1, t3), sub(t0, t2), add_i(t1, t3)]


def unfold(x):
    t0, t1, t2, t3 = add(x[0], x[2]), sub(x[0], x[2]), add(x[1], x[3]), sub(x[1], x[3])
    return [add(t0, t2), add_i(t1, t3), sub(t0, t2), sub_i(t1, t3)]


def fold2(e):
    rows = [fold(e[q]) for q in range(4)]
    cols = [fold([rows[q][m] for q in range(4)]) for m in range(4)]
    return [[cols[mc][mr] for mc in range(4)] for mr in range(4)]


def unfold2(e):
    cols = [unfold([e[q][m] for q in range(4)]) for m in range(4)]
    return [unfold([cols[m][q] for m in range(4)]) for q in range(4)]


def lanes(q):
    return slice(q * B, q * B + B)


def store_y(ya, y, row, n):
    for mr in range(4):
        for mc in range(4):
            for ri in range(2):
                at = (mr * 2 + ri) * B + row
                ya[at : at + n, lanes(mc)] = y[mr][mc][ri].astype(bf16)


def load_f(f, row, n):
    return [
        [
            tuple(
                f[(mr * 2 + ri) * B + row : (mr * 2 + ri) * B + row + n, lanes(mc)]
                for ri in range(2)
            )
            for mc in range(4)
        ]
        for mr in range(4)
    ]


ROWS = 16


def stage1(v, pr, ya, tile, place):
    n = ROWS
    for i in range(2):
        for part in range(0, 32, n):
            row = place * 32 + part
            e = []
            for q in range(4):
                line = []
                for c in range(4):
                    vr = v[q * 4 + tile, 0, part : part + n, lanes(c)].astype(f32)
                    vi = v[q * 4 + tile, 1, part : part + n, lanes(c)].astype(f32)
                    a = pr[i, 0, q * B + row : q * B + row + n, lanes(c)].astype(f32)
                    b = pr[i, 1, q * B + row : q * B + row + n, lanes(c)].astype(f32)
                    line.append((a * vr - b * vi, a * vi + b * vr))
                e.append(line)
            store_y(ya.at[i], fold2(e), row, n)


def right(ya, mats, out, dtype, place):
    rows = [(i, slice(m * B + place * 32, m * B + place * 32 + 32)) for i in range(2) for m in range(8)]
    for mc in range(4):
        lhs = jnp.concatenate(
            [
                jnp.concatenate([ya[i, at, lanes(mc)] for i, at in rows[p : p + 2]], 1)
                for p in range(0, 16, 2)
            ],
            0,
        )
        r = jnp.dot(lhs, mats[mc], preferred_element_type=f32)
        for p, (i, at) in enumerate(rows):
            out[i, at, lanes(mc)] = r[p // 2 * 32 : p // 2 * 32 + 32, lanes(p % 2)].astype(dtype)


def left_part(mats, yb, out, dtype, mr):
    at = slice(mr * 256, mr * 256 + 256)
    out[at, :] = jnp.dot(mats[mr], yb[at, :], preferred_element_type=f32).astype(dtype)


def stage2_part(f, am, ya, g):
    n = ROWS
    row = g * n
    w = unfold2(load_f(f, row, n))
    for q in range(4):
        for c in range(4):
            wr, wi = w[q][c]
            a = am[q * B + row : q * B + row + n, lanes(c)].astype(f32)
            s = 1.0 - a * lax.rsqrt(wr * wr + wi * wi + soften)
            w[q][c] = (wr * s, wi * s)
    store_y(ya, fold2(w), row, n)


def middle(mat_l, mat_r, am, ya, yb, ff, before_second):
    def lead(i, g):
        left_part(mat_l, yb.at[i], ff.at[i], f32, g)

    def back(i, g):
        left_part(mat_r, ya.at[i], yb.at[i], bf16, g)

    def misfit(i, g):
        for h in (2 * g, 2 * g + 1):
            stage2_part(ff.at[i], am.at[i], ya.at[i], h)

    for g in range(4):
        lead(0, g)
    for g in range(4):
        lead(1, g)
        misfit(0, g)
    before_second()
    for g in range(4):
        back(0, g)
        misfit(1, g)
    for g in range(4):
        back(1, g)


def stage3(f, pr, g, place):
    n = ROWS
    for part in range(0, 32, n):
        row = place * 32 + part
        tot = None
        for i in range(2):
            w = unfold2(load_f(f.at[i], row, n))
            new = []
            for q in range(4):
                for c in range(4):
                    a = pr[i, 0, q * B + row : q * B + row + n, lanes(c)].astype(f32)
                    b = pr[i, 1, q * B + row : q * B + row + n, lanes(c)].astype(f32)
                    br, bi = w[q][c]
                    new.append((a * br + b * bi, a * bi - b * br))
            tot = new if tot is None else [add(p, q) for p, q in zip(tot, new)]
        for q in range(4):
            for c in range(4):
                for ri in range(2):
                    g[q, ri, part : part + n, lanes(c)] = tot[q * 4 + c][ri].astype(g.dtype)


def one_hot(offset, order, transpose):
    a = lax.broadcasted_iota(jnp.int32, (N, N), 0)
    b = lax.broadcasted_iota(jnp.int32, (N, N), 1)
    if transpose:
        return jnp.where(a == ((b + offset) & (N - 1)), 1.0, 0.0).astype(bf16)
    return jnp.where(b == (((a ^ order) + offset) & (N - 1)), 1.0, 0.0).astype(bf16)


def make_hot(off, order, hot):
    hot[0] = one_hot(off[0:1, 0:1], order, False)
    hot[1] = one_hot(off[8:9, 0:1], order, True)


def roll_plane(src, hot, tmp, dst):
    for h in range(2):
        sl = slice(h * 256, h * 256 + 256)
        tmp[sl, :] = jnp.dot(hot[0, sl, :], src[...], preferred_element_type=f32).astype(bf16)
    for h in range(2):
        sl = slice(h * 256, h * 256 + 256)
        dst[sl, :] = jnp.dot(tmp[sl, :], hot[1], preferred_element_type=f32).astype(bf16)


SEG = 320
DEPTH = 3 * SEG


def net_weights(conv_first, bias_first, conv_middle, bias_middle, conv_last, pad, w_first, w_mid, w_last, bias):
    pad[...] = jnp.zeros_like(pad)
    for layer in range(2):
        for p in range(3):
            for t in range(3):
                pad[p * 3 + t, :, 0:32] = conv_middle[layer, p, t].astype(f32)
        turned = [
            [[pltpu.roll(pad[p * 3 + t], 32 * m, 1) if m else pad[p * 3 + t] for m in range(4)] for t in range(3)]
            for p in range(3)
        ]
        for k in range(8):
            blocks = [None] * 8
            for t in range(3):
                for p in range(3):
                    at = t * SEG + (k + p) * 32
                    piece = turned[p][t][at // 32 % 4]
                    held = blocks[at // B]
                    blocks[at // B] = piece if held is None else held + piece
            for j in range(8):
                value = jnp.zeros((32, B), f32) if blocks[j] is None else blocks[j]
                w_mid[layer, k * 32 : k * 32 + 32, lanes(j)] = value.astype(bf16)
    pad[...] = jnp.zeros_like(pad)
    square = pad.at[0:4]
    for p in range(3):
        for t in range(3):
            at = (p * 3 + t) * 8
            square[at // 32, at % 32 : at % 32 + 2, 0:32] = conv_first[p, t].astype(f32)
    flipped = jnp.transpose(pad[0:4].reshape(B, B))[0:32, :]
    group = lax.broadcasted_iota(jnp.int32, (32, B), 1) >> 3
    base = jnp.zeros((32, 256), f32)
    for p in range(3):
        for t in range(3):
            piece = jnp.where(group == p * 3 + t, flipped, 0.0)
            wide = jnp.concatenate([piece, jnp.zeros((32, B), f32)], 1)
            base = base + pltpu.roll(wide, (t * 48 + 6 + 2 * p - (p * 3 + t) * 8) % 256, 1)
    for k in range(16):
        w_first[k * 32 : k * 32 + 32, :] = (pltpu.roll(base, 2 * k, 1) if k else base).astype(bf16)
    pad[...] = jnp.zeros_like(pad)
    base = jnp.zeros((8, 640), f32)
    for p in range(3):
        pad[p, 0:3, 0:32] = conv_last[p].astype(f32)
        wide = jnp.concatenate([pad[p, 0:8, :], jnp.zeros((8, 512), f32)], 1)
        base = base + (pltpu.roll(wide, 32 * p, 1) if p else wide)
    row = lax.broadcasted_iota(jnp.int32, (16, N), 0)
    taps = [jnp.zeros((16, N), f32) for t in range(3)]
    for k in range(16):
        turned_k = (pltpu.roll(base, (32 * (k - 1)) % 640, 1) if k != 1 else base)[:, 0:N]
        for t in range(3):
            taps[t] = jnp.where(row == k, jnp.broadcast_to(turned_k[t : t + 1, :], (16, N)), taps[t])
    for t in range(3):
        w_last[t * 16 : t * 16 + 16, :] = taps[t].astype(bf16)
    eye = lax.broadcasted_iota(jnp.int32, (32, 32), 0) == lax.broadcasted_iota(jnp.int32, (32, 32), 1)
    for i in range(3):
        line = bias_first[0:1, :] if i == 0 else bias_middle[i - 1 : i, :]
        column = jnp.sum(jnp.where(eye, jnp.broadcast_to(line, (32, 32)), 0.0), axis=1, keepdims=True)
        bias[i] = jnp.broadcast_to(column, (32, B))


def make_perm(slot_angle, perm):
    r = lax.broadcasted_iota(jnp.int32, (B, B), 0)
    m = lax.broadcasted_iota(jnp.int32, (B, B), 1)
    angle = jnp.zeros((B, B), jnp.int32)
    for j in range(16):
        angle = jnp.where((m >> 3) == j, slot_angle[j], angle)
    hit = ((r >> 5) == (m & 3)) & ((r & 1) == ((m >> 2) & 1)) & (((r >> 1) & 15) == angle)
    perm[...] = jnp.where(hit, 1.0, 0.0).astype(bf16)


def taps_of(value):
    width = value.shape[1]
    lane = lax.broadcasted_iota(jnp.int32, value.shape, 1)
    before = jnp.where(lane == 0, 0.0, pltpu.roll(value, 1, 1))
    after = jnp.where(lane == width - 1, 0.0, pltpu.roll(value, width - 1, 1))
    return before, value, after


def net_layer_out(out, bias_i, b, u, dst, last):
    for k in range(8):
        block = jnp.concatenate(
            [jnp.maximum(out[k * 32 : k * 32 + 32, lanes(q)] + bias_i, 0.0) for q in range(4)], 1
        )
        if last:
            dst[u, (b * 8 + k) * 32 : (b * 8 + k) * 32 + 32, :] = block.astype(bf16)
            continue
        for t, piece in enumerate(taps_of(block)):
            piece = piece.astype(bf16)
            at = t * SEG + (k + 1) * 32
            dst[u, b, at : at + 32, :] = piece
            if b == 0 and k == 7:
                dst[u, 1, t * SEG : t * SEG + 32, :] = piece
            if b == 1 and k == 0:
                dst[u, 0, t * SEG + 288 : t * SEG + 320, :] = piece


def net_clear(ha, hb):
    for h in (ha, hb):
        for u in range(4):
            for t in range(3):
                zero = jnp.zeros((32, N), bf16)
                h[u, 0, t * SEG : t * SEG + 32, :] = zero
                h[u, 1, t * SEG + 288 : t * SEG + 320, :] = zero
            for b in range(2):
                h[u, b, DEPTH:1024, :] = jnp.zeros((1024 - DEPTH, N), bf16)


def net_run(nb, perm, w_first, w_mid, w_last, bias, ordered, ha, hb, hc, out_ref):
    ordered[...] = jnp.dot(perm[...], nb[...].reshape(B, N), preferred_element_type=f32)

    def first(u, _):
        mine = ordered[pl.ds(pl.multiple_of(u * 32, 32), 32), :]
        zero = jnp.zeros((8, N), f32)
        parts = []
        for piece in taps_of(mine):
            parts += [zero, piece, zero]
        stacked = jnp.concatenate(parts + [jnp.zeros((256 - 144, N), f32)], 0).astype(bf16)
        for b in range(2):
            out = jnp.dot(w_first[b * 256 : b * 256 + 256, :], stacked, preferred_element_type=f32)
            net_layer_out(out, bias[0], b, u, ha, False)
        return 0

    lax.fori_loop(0, 4, first, 0)
    for layer in range(2):
        src, dst = (ha, hb) if layer == 0 else (hb, hc)

        def middle(u, _):
            for b in range(2):
                out = jnp.dot(w_mid[layer], src[u, b], preferred_element_type=f32)
                net_layer_out(out, bias[layer + 1], b, u, dst, layer == 1)
            return 0

        lax.fori_loop(0, 4, middle, 0)

    def final(u, _):
        out = jnp.dot(w_last[...], hc[u], preferred_element_type=f32)
        before = taps_of(out[0:16, :])[0]
        after = taps_of(out[32:48, :])[2]
        at = pl.multiple_of(128 + u * 16, 16)
        out_ref[pl.ds(at, 16), :] = before + out[16:32, :] + after
        return 0

    lax.fori_loop(0, 4, final, 0)


def main_kernel(
    obj,
    probe_hbm,
    amps_hbm,
    off,
    mats_hbm,
    slot_angle,
    conv_first,
    bias_first,
    conv_middle,
    bias_middle,
    conv_last,
    out,
    mats,
    pad,
    w_first,
    w_mid,
    w_last,
    bias,
    perm,
    ordered,
    ha,
    hb,
    hc,
    view,
    probe_in,
    amps_in,
    probe16,
    amp16,
    amp_send,
    amp_recv,
    off_own,
    off_send,
    off_recv,
    hot,
    tmp,
    pr,
    am,
    ya,
    yb,
    ff,
    x_obj,
    g_send,
    g_recv,
    g_own,
    sa,
    sb,
    ra,
    rb,
    total,
    as_send,
    nb,
    local_sem,
    x_sem,
    ag_recv,
    ring_send,
    sib_send,
    gs_sem,
    gr_sem,
    sa_sem,
    sb_sem,
    ra_sem,
    rb_sem,
    aa_send,
    aa_recv,
):
    pos = lax.axis_index("pos")
    ang = lax.axis_index("ang")
    c = lax.rem(pos, 2)
    s = lax.rem(pos // 2, 2)
    y = pos // 4
    me = 2 * s + c
    up = lax.rem(y + 1, 4)
    down = lax.rem(y + 3, 4)
    far = lax.rem(y + 2, 4)

    def at(yy, xx, cc):
        return yy * 4 + xx * 2 + cc

    dev_up = (ang, at(up, s, c))
    dev_down = (ang, at(down, s, c))
    dev_far = (ang, at(far, s, c))
    dev_x = (ang, at(y, 1 - s, c))
    dev_sib = (ang, at(y, s, 1 - c))
    step_size = learning / 16

    def put_obj(slot, value):
        for ri in range(2):
            out[pl.ds(pl.multiple_of(slot * 64 + ri * 32, 32), 32), :] = value[ri]

    def rc(src, dst, send, recv, dev):
        return pltpu.make_async_remote_copy(
            src_ref=src, dst_ref=dst, send_sem=send, recv_sem=recv, device_id=dev,
            device_id_type=MESH,
        )

    def arrived(dst, recv):
        rc(dst, dst, recv, recv, dev_x).wait_recv()

    def left_dev(src, send):
        rc(src, src, send, send, dev_x).wait_send()

    cp_probe = pltpu.make_async_copy(probe_hbm, probe_in, local_sem.at[0])
    cp_amps = pltpu.make_async_copy(amps_hbm, amps_in, local_sem.at[1])
    cp_mats = pltpu.make_async_copy(mats_hbm.at[0], mats.at[0], local_sem.at[2])
    cp_mats_mine = pltpu.make_async_copy(mats_hbm.at[me], mats.at[1], local_sem.at[3])
    cp_amps.start()
    cp_probe.start()
    cp_mats.start()
    cp_mats_mine.start()
    mat_l, mat_r = mats.at[0, 0], mats.at[0, 1]
    row_l, row_r = mats.at[1, 0], mats.at[1, 1]

    barrier = pltpu.get_barrier_semaphore()
    peers = [dev_up, dev_down, dev_far, dev_x, dev_sib]
    peers += [(ang, at(yy, 1 - s, c)) for yy in (up, down, far)]
    for dev in peers:
        pl.semaphore_signal(barrier, inc=1, device_id=dev, device_id_type=MESH)
    for d in range(1, 8):
        pl.semaphore_signal(
            barrier, inc=1, device_id=(lax.rem(ang + d, 8), pos), device_id_type=MESH
        )

    own = at(y, s, c)
    other = at(y, 1 - s, c)
    view[0, own] = obj[s].astype(bf16)
    x_obj[...] = obj[1 - s].astype(bf16)
    for i, (ref, slot) in enumerate(((off_own, s), (off_send, 1 - s))):
        for k in range(2):
            value = jnp.where(slot == 0, off[0, 0, k], off[1, 0, k])
            ref[k * 8 : k * 8 + 8, :] = jnp.full((8, 128), value, jnp.int32)

    pl.semaphore_wait(barrier, 15)

    rc(x_obj, view.at[0, own], x_sem.at[0], ag_recv.at[0, own], dev_x).start()
    rc(off_send, off_recv, x_sem.at[1], x_sem.at[2], dev_x).start()

    around = ((up, dev_up), (down, dev_down), (far, dev_far))

    def ag_start(k, xx):
        tile = at(y, xx, c)
        ref = view.at[k, tile]
        for d, (_, dev) in enumerate(around):
            rc(ref, ref, ring_send.at[k, xx, d], ag_recv.at[k, tile], dev).start()
        rc(ref, ref, sib_send.at[k, 3, xx], ag_recv.at[k, tile], dev_sib).start()

    def ag_relay(k, xx):
        for d, (yy, _) in enumerate(around):
            tile = at(yy, xx, c)
            ref = view.at[k, tile]
            arrived(ref, ag_recv.at[k, tile])
            rc(ref, ref, sib_send.at[k, d, xx], ag_recv.at[k, tile], dev_sib).start()

    def ag_rest(k, xx):
        for yy in range(4):
            tile = at(yy, xx, 1 - c)
            arrived(view.at[k, tile], ag_recv.at[k, tile])

    def ag_sent(k):
        for xx in range(2):
            tile = at(y, xx, c)
            for d in range(3):
                left_dev(view.at[k, tile], ring_send.at[k, xx, d])
            for d, yy in enumerate((up, down, far, y)):
                left_dev(view.at[k, at(yy, xx, c)], sib_send.at[k, d, xx])

    ag_start(0, s)
    cp_amps.wait()
    amp_send[...] = amps_in[1 - s, 0].astype(bf16)
    cp_amp_x = rc(amp_send, amp_recv, x_sem.at[3], x_sem.at[4], dev_x)
    cp_amp_x.start()
    amp16[...] = amps_in[s, 0].astype(bf16)
    arrived(view.at[0, other], ag_recv.at[0, other])
    ag_start(0, 1 - s)
    cp_probe.wait()
    probe16[...] = probe_in[...].astype(bf16)
    make_hot(off_own, 32 * me, hot.at[0])
    roll_plane(probe16.at[0], hot.at[0], tmp, pr.at[0, 0])
    roll_plane(probe16.at[1], hot.at[0], tmp, pr.at[0, 1])
    ag_relay(0, s)
    arrived(off_recv, x_sem.at[2])
    make_hot(off_recv, 32 * me, hot.at[1])
    roll_plane(probe16.at[0], hot.at[1], tmp, pr.at[1, 0])
    ag_relay(0, 1 - s)
    roll_plane(probe16.at[1], hot.at[1], tmp, pr.at[1, 1])
    cp_mats.wait()
    cp_mats_mine.wait()

    cols = (s, 1 - s)
    tiles = (me, 2 * s + 1 - c, 2 * (1 - s) + c, 2 * (1 - s) + 1 - c)

    def enter(k, *places):
        for place in places:
            stage1(view.at[k], pr, ya, tiles[place], place)
        for place in places:
            right(ya, mat_r, yb, bf16, place)

    def leave(g, place):
        right(yb, mat_l, ff, f32, place)
        stage3(ff, pr, g, place)

    def before_second(k):
        if k == 0:
            arrived(amp_recv, x_sem.at[4])
            roll_plane(amp_recv, hot.at[1], tmp, am.at[1])

    for k in range(2):
        if k == 1:
            ag_relay(k, s)
        enter(k, 0)
        if k == 1:
            ag_relay(k, 1 - s)
        ag_rest(k, s)
        enter(k, 1, 2)
        ag_rest(k, 1 - s)
        enter(k, 3)
        if k == 0:
            roll_plane(amp16, hot.at[0], tmp, am.at[0])
        middle(row_l, row_r, am, ya, yb, ff, functools.partial(before_second, k))
        order = (0, 1) if k == 0 else (1, 0)
        for o in order:
            leave(g_send.at[k, o], 2 * o + 1)
            rc(g_send.at[k, o], g_recv.at[k, o], gs_sem.at[k, o], gr_sem.at[k, o],
               dev_sib).start()

        def comb(yy, o):
            return g_own[o, yy] + g_recv[k, o, yy].astype(f32)

        if k == 0:
            for o in order:
                leave(g_own.at[o], 2 * o)
                arrived(g_recv.at[0, o], gr_sem.at[0, o])
                for d, (yy, dev) in ((2, around[2]), (0, around[0]), (1, around[1])):
                    sa[d, o] = comb(yy, o).astype(bf16)
                    rc(sa.at[d, o], ra.at[d, o], sa_sem.at[d, o], ra_sem.at[d, o], dev).start()
            ag_sent(0)
            net_weights(
                conv_first, bias_first, conv_middle, bias_middle, conv_last, pad, w_first, w_mid,
                w_last, bias,
            )
            for o in order:
                sum_x = comb(y, o)
                for d in range(3):
                    arrived(ra.at[d, o], ra_sem.at[d, o])
                    sum_x = sum_x + ra[d, o].astype(f32)
                total[o] = sum_x
                if o == 0:
                    view[1, own] = (obj[s] - step_size * sum_x).astype(bf16)
                else:
                    view[1, other] = (view[0, other].astype(f32) - step_size * sum_x).astype(bf16)
                ag_start(1, cols[o])
            make_perm(slot_angle, perm)
            net_clear(ha, hb)
            for d in range(3):
                for o in range(2):
                    left_dev(sa.at[d, o], sa_sem.at[d, o])
        else:
            for o in order:
                leave(g_own.at[o], 2 * o)
                arrived(g_recv.at[1, o], gr_sem.at[1, o])
                if o == 1:
                    sb[1, 3] = (comb(y, 1) + total[1]).astype(bf16)
                    rc(sb.at[1, 3], rb.at[1, 3], sb_sem.at[1, 3], rb_sem.at[1, 3], dev_x).start()
                for d, (yy, _) in ((2, around[2]), (0, around[0]), (1, around[1])):
                    sb[o, d] = comb(yy, o).astype(bf16)
                    rc(sb.at[o, d], rb.at[o, d], sb_sem.at[o, d], rb_sem.at[o, d],
                       (ang, at(yy, cols[o], c))).start()
            ag_sent(1)
            for d in range(4):
                arrived(rb.at[1, d], rb_sem.at[1, d])
            theirs = (
                rb[1, 0].astype(f32) + rb[1, 1].astype(f32) + rb[1, 2].astype(f32)
                + rb[1, 3].astype(f32)
            )
            put_obj(1 - s, obj[1 - s] - step_size * theirs)
            mine = comb(y, 0) + total[0]
            for d in range(3):
                arrived(rb.at[0, d], rb_sem.at[0, d])
                mine = mine + rb[0, d].astype(f32)
            put_obj(s, obj[s] - step_size * mine)
        for o in range(2):
            left_dev(g_send.at[k, o], gs_sem.at[k, o])

    for g in range(8):
        as_send[g] = jnp.concatenate(
            [out[q * 32 + g * 4 : q * 32 + g * 4 + 4, :] for q in range(4)], 0
        ).astype(bf16)

    def a2a(d):
        to = lax.rem(ang + d, 8)
        return rc(as_send.at[to], nb.at[ang], aa_send.at[d], aa_recv.at[ang], (to, pos))

    for d in range(1, 8):
        a2a(d).start()
    nb[ang] = as_send[ang]
    for d in range(1, 8):
        frm = lax.rem(ang + d, 8)
        arrived(nb.at[frm], aa_recv.at[frm])
    net_run(nb, perm, w_first, w_mid, w_last, bias, ordered, ha, hb, hc, out)
    for d in range(1, 8):
        a2a(d).wait_send()
    for o in range(2):
        for d in range(3 + o):
            left_dev(sb.at[o, d], sb_sem.at[o, d])
    left_dev(x_obj, x_sem.at[0])
    left_dev(off_send, x_sem.at[1])
    cp_amp_x.wait_send()


def split_kernel(both, obj_out, proj_out):
    obj_out[...] = both[0:128]
    proj_out[...] = both[128:192]


def split(both):
    vm = pl.BlockSpec(memory_space=pltpu.VMEM)
    return pl.pallas_call(
        split_kernel,
        out_shape=(
            jax.ShapeDtypeStruct((128, N), f32),
            jax.ShapeDtypeStruct((64, N), f32),
        ),
        in_specs=[vm],
        out_specs=(vm, vm),
    )(both)


def sweeps(
    object_init,
    probe_field,
    amplitudes,
    offsets,
    slot_angle,
    conv_first,
    bias_first,
    conv_middle,
    bias_middle,
    conv_last,
):
    mats = make_tables()
    vm = pl.BlockSpec(memory_space=pltpu.VMEM)
    hbm = pl.BlockSpec(memory_space=pltpu.HBM)
    smem = pl.BlockSpec(memory_space=pltpu.SMEM)
    tile = (2, 32, N)
    scratch = [
        pltpu.VMEM((2, 2, 4, 256, 256), bf16),
        pltpu.VMEM((9, 32, B), f32),
        pltpu.VMEM((N, 256), bf16),
        pltpu.VMEM((2, 256, 1024), bf16),
        pltpu.VMEM((48, N), bf16),
        pltpu.VMEM((3, 32, B), f32),
        pltpu.VMEM((B, B), bf16),
        pltpu.VMEM((B, N), f32),
        pltpu.VMEM((4, 2, 1024, N), bf16),
        pltpu.VMEM((4, 2, 1024, N), bf16),
        pltpu.VMEM((4, N, N), bf16),
        pltpu.VMEM((2, 16) + tile, bf16),
        pltpu.VMEM((2, N, N), f32),
        pltpu.VMEM((2, 1, N, N), f32),
        pltpu.VMEM((2, N, N), bf16),
        pltpu.VMEM((N, N), bf16),
        pltpu.VMEM((N, N), bf16),
        pltpu.VMEM((N, N), bf16),
        pltpu.VMEM((16, 128), jnp.int32),
        pltpu.VMEM((16, 128), jnp.int32),
        pltpu.VMEM((16, 128), jnp.int32),
        pltpu.VMEM((2, 2, N, N), bf16),
        pltpu.VMEM((N, N), bf16),
        pltpu.VMEM((2, 2, N, N), bf16),
        pltpu.VMEM((2, N, N), bf16),
        pltpu.VMEM((2, 2 * N, N), bf16),
        pltpu.VMEM((2, 2 * N, N), bf16),
        pltpu.VMEM((2, 2 * N, N), f32),
        pltpu.VMEM(tile, bf16),
        pltpu.VMEM((2, 2, 4) + tile, bf16),
        pltpu.VMEM((2, 2, 4) + tile, bf16),
        pltpu.VMEM((2, 4) + tile, f32),
        pltpu.VMEM((3, 2) + tile, bf16),
        pltpu.VMEM((2, 4) + tile, bf16),
        pltpu.VMEM((3, 2) + tile, bf16),
        pltpu.VMEM((2, 4) + tile, bf16),
        pltpu.VMEM((2,) + tile, f32),
        pltpu.VMEM((8, 16, N), bf16),
        pltpu.VMEM((8, 16, N), bf16),
        pltpu.SemaphoreType.DMA((4,)),
        pltpu.SemaphoreType.DMA((5,)),
        pltpu.SemaphoreType.DMA((2, 16)),
        pltpu.SemaphoreType.DMA((2, 2, 3)),
        pltpu.SemaphoreType.DMA((2, 4, 2)),
        pltpu.SemaphoreType.DMA((2, 2)),
        pltpu.SemaphoreType.DMA((2, 2)),
        pltpu.SemaphoreType.DMA((3, 2)),
        pltpu.SemaphoreType.DMA((2, 4)),
        pltpu.SemaphoreType.DMA((3, 2)),
        pltpu.SemaphoreType.DMA((2, 4)),
        pltpu.SemaphoreType.DMA((8,)),
        pltpu.SemaphoreType.DMA((8,)),
    ]
    return pl.pallas_call(
        main_kernel,
        out_shape=jax.ShapeDtypeStruct((192, N), f32),
        in_specs=[vm, hbm, hbm, smem, hbm, smem] + [vm] * 5,
        out_specs=vm,
        scratch_shapes=scratch,
        compiler_params=pltpu.CompilerParams(
            collective_id=0, has_side_effects=True, vmem_limit_bytes=60 << 20
        ),
        cost_estimate=pl.CostEstimate(
            flops=12_000_000_000, bytes_accessed=8_000_000, transcendentals=1_000_000
        ),
    )(
        object_init,
        probe_field,
        amplitudes,
        offsets,
        jnp.asarray(mats),
        slot_angle,
        conv_first.transpose(0, 1, 3, 2),
        bias_first.reshape(1, 32),
        conv_middle,
        bias_middle,
        conv_last,
    )


def on_device(
    object_init,
    probe_field,
    amplitudes,
    offsets,
    slot_angle,
    conv_first,
    bias_first,
    conv_middle,
    bias_middle,
    conv_last,
):
    both = sweeps(
        object_init,
        probe_field,
        amplitudes,
        offsets,
        slot_angle,
        conv_first,
        bias_first,
        conv_middle,
        bias_middle,
        conv_last,
    )
    obj_new, projections = split(both)
    return (obj_new.reshape(2, 2, 32, N), projections.reshape(1, 1, 4, 16, N))


def solution(mesh):
    return jax.shard_map(
        on_device,
        mesh=mesh,
        in_specs=(
            P("ang", None, "pos", None),
            P(),
            P("ang", "pos", None, None),
            P("ang", "pos", None),
            P(),
            P(),
            P(),
            P(),
            P(),
            P(),
        ),
        out_specs=(P("ang", None, "pos", None), P("pos", "ang", None, None, None)),
        check_vma=False,
    )
```

```python
import functools

import jax
import jax.numpy as jnp
import ml_dtypes
import numpy as np
from jax import lax
from jax.experimental import pallas as pl
from jax.experimental.pallas import tpu as pltpu
from jax.sharding import PartitionSpec as P

soften = 0.25
learning = 1.5
N = 512
B = 128
f32 = jnp.float32
bf16 = jnp.bfloat16
MESH = pl.DeviceIdType.MESH


def make_tables():
    f = np.arange(N)
    g = np.where(f < N // 2, f, f - N).astype(np.float64)
    lam = np.exp(-3j * np.pi * g * g / (4 * N))
    d = np.arange(B)[:, None] - np.arange(B)[None, :]
    blocks = []
    for m in range(4):
        fm = np.arange(m, N, 4)
        c = (lam[fm] * np.exp(2j * np.pi * fm * d[:, :, None] / N)).sum(-1) / N
        blocks.append(np.block([[c.real, -c.imag], [c.imag, c.real]]))
    left = np.stack(blocks)
    pair = np.stack([left, np.swapaxes(left, 1, 2)]).astype(ml_dtypes.bfloat16)
    orders = [np.arange(256) ^ (32 * k) for k in range(4)]
    return np.stack([pair[:, :, order][:, :, :, order] for order in orders])


def add(a, b):
    return (a[0] + b[0], a[1] + b[1])


def sub(a, b):
    return (a[0] - b[0], a[1] - b[1])


def add_i(a, b):
    return (a[0] - b[1], a[1] + b[0])


def sub_i(a, b):
    return (a[0] + b[1], a[1] - b[0])


def fold(x):
    t0, t1, t2, t3 = add(x[0], x[2]), sub(x[0], x[2]), add(x[1], x[3]), sub(x[1], x[3])
    return [add(t0, t2), sub_i(t1, t3), sub(t0, t2), add_i(t1, t3)]


def unfold(x):
    t0, t1, t2, t3 = add(x[0], x[2]), sub(x[0], x[2]), add(x[1], x[3]), sub(x[1], x[3])
    return [add(t0, t2), add_i(t1, t3), sub(t0, t2), sub_i(t1, t3)]


def fold2(e):
    rows = [fold(e[q]) for q in range(4)]
    cols = [fold([rows[q][m] for q in range(4)]) for m in range(4)]
    return [[cols[mc][mr] for mc in range(4)] for mr in range(4)]


def unfold2(e):
    cols = [unfold([e[q][m] for q in range(4)]) for m in range(4)]
    return [unfold([cols[m][q] for m in range(4)]) for q in range(4)]


def lanes(q):
    return slice(q * B, q * B + B)


def store_y(ya, y, row, n):
    for mr in range(4):
        for mc in range(4):
            for ri in range(2):
                at = (mr * 2 + ri) * B + row
                ya[at : at + n, lanes(mc)] = y[mr][mc][ri].astype(bf16)


def load_f(f, row, n):
    return [
        [
            tuple(
                f[(mr * 2 + ri) * B + row : (mr * 2 + ri) * B + row + n, lanes(mc)]
                for ri in range(2)
            )
            for mc in range(4)
        ]
        for mr in range(4)
    ]


ROWS = 16


def stage1(v, pr, ya, tile, place):
    n = ROWS
    for i in range(2):
        for part in range(0, 32, n):
            row = place * 32 + part
            e = []
            for q in range(4):
                line = []
                for c in range(4):
                    vr = v[q * 4 + tile, 0, part : part + n, lanes(c)].astype(f32)
                    vi = v[q * 4 + tile, 1, part : part + n, lanes(c)].astype(f32)
                    a = pr[i, 0, q * B + row : q * B + row + n, lanes(c)].astype(f32)
                    b = pr[i, 1, q * B + row : q * B + row + n, lanes(c)].astype(f32)
                    line.append((a * vr - b * vi, a * vi + b * vr))
                e.append(line)
            store_y(ya.at[i], fold2(e), row, n)


def right(ya, mats, out, dtype, place):
    rows = [(i, slice(m * B + place * 32, m * B + place * 32 + 32)) for i in range(2) for m in range(8)]
    for mc in range(4):
        lhs = jnp.concatenate(
            [
                jnp.concatenate([ya[i, at, lanes(mc)] for i, at in rows[p : p + 2]], 1)
                for p in range(0, 16, 2)
            ],
            0,
        )
        r = jnp.dot(lhs, mats[mc], preferred_element_type=f32)
        for p, (i, at) in enumerate(rows):
            out[i, at, lanes(mc)] = r[p // 2 * 32 : p // 2 * 32 + 32, lanes(p % 2)].astype(dtype)


def left_part(mats, yb, out, dtype, mr):
    at = slice(mr * 256, mr * 256 + 256)
    out[at, :] = jnp.dot(mats[mr], yb[at, :], preferred_element_type=f32).astype(dtype)


def stage2_part(f, am, ya, g):
    n = ROWS
    row = g * n
    w = unfold2(load_f(f, row, n))
    for q in range(4):
        for c in range(4):
            wr, wi = w[q][c]
            a = am[q * B + row : q * B + row + n, lanes(c)].astype(f32)
            s = 1.0 - a * lax.rsqrt(wr * wr + wi * wi + soften)
            w[q][c] = (wr * s, wi * s)
    store_y(ya, fold2(w), row, n)


def middle(mat_l, mat_r, am, ya, yb, ff, before_second):
    def lead(i, g):
        left_part(mat_l, yb.at[i], ff.at[i], f32, g)

    def back(i, g):
        left_part(mat_r, ya.at[i], yb.at[i], bf16, g)

    def misfit(i, g):
        for h in (2 * g, 2 * g + 1):
            stage2_part(ff.at[i], am.at[i], ya.at[i], h)

    for g in range(4):
        lead(0, g)
    for g in range(4):
        lead(1, g)
        misfit(0, g)
    before_second()
    for g in range(4):
        back(0, g)
        misfit(1, g)
    for g in range(4):
        back(1, g)


def stage3(f, pr, g, place):
    n = ROWS
    for part in range(0, 32, n):
        row = place * 32 + part
        tot = None
        for i in range(2):
            w = unfold2(load_f(f.at[i], row, n))
            new = []
            for q in range(4):
                for c in range(4):
                    a = pr[i, 0, q * B + row : q * B + row + n, lanes(c)].astype(f32)
                    b = pr[i, 1, q * B + row : q * B + row + n, lanes(c)].astype(f32)
                    br, bi = w[q][c]
                    new.append((a * br + b * bi, a * bi - b * br))
            tot = new if tot is None else [add(p, q) for p, q in zip(tot, new)]
        for q in range(4):
            for c in range(4):
                for ri in range(2):
                    g[q, ri, part : part + n, lanes(c)] = tot[q * 4 + c][ri].astype(g.dtype)


def one_hot(offset, order, transpose):
    a = lax.broadcasted_iota(jnp.int32, (N, N), 0)
    b = lax.broadcasted_iota(jnp.int32, (N, N), 1)
    if transpose:
        return jnp.where(a == ((b + offset) & (N - 1)), 1.0, 0.0).astype(bf16)
    return jnp.where(b == (((a ^ order) + offset) & (N - 1)), 1.0, 0.0).astype(bf16)


def make_hot(off, order, hot):
    hot[0] = one_hot(off[0:1, 0:1], order, False)
    hot[1] = one_hot(off[8:9, 0:1], order, True)


def roll_plane(src, hot, tmp, dst):
    for h in range(2):
        sl = slice(h * 256, h * 256 + 256)
        tmp[sl, :] = jnp.dot(hot[0, sl, :], src[...], preferred_element_type=f32).astype(bf16)
    for h in range(2):
        sl = slice(h * 256, h * 256 + 256)
        dst[sl, :] = jnp.dot(tmp[sl, :], hot[1], preferred_element_type=f32).astype(bf16)


SEG = 320
DEPTH = 3 * SEG


def net_weights(conv_first, bias_first, conv_middle, bias_middle, conv_last, pad, w_first, w_mid, w_last, bias):
    pad[...] = jnp.zeros_like(pad)
    for layer in range(2):
        for p in range(3):
            for t in range(3):
                pad[p * 3 + t, :, 0:32] = conv_middle[layer, p, t].astype(f32)
        turned = [
            [[pltpu.roll(pad[p * 3 + t], 32 * m, 1) if m else pad[p * 3 + t] for m in range(4)] for t in range(3)]
            for p in range(3)
        ]
        for k in range(8):
            blocks = [None] * 8
            for t in range(3):
                for p in range(3):
                    at = t * SEG + (k + p) * 32
                    piece = turned[p][t][at // 32 % 4]
                    held = blocks[at // B]
                    blocks[at // B] = piece if held is None else held + piece
            for j in range(8):
                value = jnp.zeros((32, B), f32) if blocks[j] is None else blocks[j]
                w_mid[layer, k * 32 : k * 32 + 32, lanes(j)] = value.astype(bf16)
    pad[...] = jnp.zeros_like(pad)
    square = pad.at[0:4]
    for p in range(3):
        for t in range(3):
            at = (p * 3 + t) * 8
            square[at // 32, at % 32 : at % 32 + 2, 0:32] = conv_first[p, t].astype(f32)
    flipped = jnp.transpose(pad[0:4].reshape(B, B))[0:32, :]
    group = lax.broadcasted_iota(jnp.int32, (32, B), 1) >> 3
    base = jnp.zeros((32, 256), f32)
    for p in range(3):
        for t in range(3):
            piece = jnp.where(group == p * 3 + t, flipped, 0.0)
            wide = jnp.concatenate([piece, jnp.zeros((32, B), f32)], 1)
            base = base + pltpu.roll(wide, (t * 48 + 6 + 2 * p - (p * 3 + t) * 8) % 256, 1)
    for k in range(16):
        w_first[k * 32 : k * 32 + 32, :] = (pltpu.roll(base, 2 * k, 1) if k else base).astype(bf16)
    pad[...] = jnp.zeros_like(pad)
    base = jnp.zeros((8, 640), f32)
    for p in range(3):
        pad[p, 0:3, 0:32] = conv_last[p].astype(f32)
        wide = jnp.concatenate([pad[p, 0:8, :], jnp.zeros((8, 512), f32)], 1)
        base = base + (pltpu.roll(wide, 32 * p, 1) if p else wide)
    row = lax.broadcasted_iota(jnp.int32, (16, N), 0)
    taps = [jnp.zeros((16, N), f32) for t in range(3)]
    for k in range(16):
        turned_k = (pltpu.roll(base, (32 * (k - 1)) % 640, 1) if k != 1 else base)[:, 0:N]
        for t in range(3):
            taps[t] = jnp.where(row == k, jnp.broadcast_to(turned_k[t : t + 1, :], (16, N)), taps[t])
    for t in range(3):
        w_last[t * 16 : t * 16 + 16, :] = taps[t].astype(bf16)
    eye = lax.broadcasted_iota(jnp.int32, (32, 32), 0) == lax.broadcasted_iota(jnp.int32, (32, 32), 1)
    for i in range(3):
        line = bias_first[0:1, :] if i == 0 else bias_middle[i - 1 : i, :]
        column = jnp.sum(jnp.where(eye, jnp.broadcast_to(line, (32, 32)), 0.0), axis=1, keepdims=True)
        bias[i] = jnp.broadcast_to(column, (32, B))


def make_perm(slot_angle, perm):
    r = lax.broadcasted_iota(jnp.int32, (B, B), 0)
    m = lax.broadcasted_iota(jnp.int32, (B, B), 1)
    angle = jnp.zeros((B, B), jnp.int32)
    for j in range(16):
        angle = jnp.where((m >> 3) == j, slot_angle[j], angle)
    hit = ((r >> 5) == (m & 3)) & ((r & 1) == ((m >> 2) & 1)) & (((r >> 1) & 15) == angle)
    perm[...] = jnp.where(hit, 1.0, 0.0).astype(bf16)


def taps_of(value):
    width = value.shape[1]
    lane = lax.broadcasted_iota(jnp.int32, value.shape, 1)
    before = jnp.where(lane == 0, 0.0, pltpu.roll(value, 1, 1))
    after = jnp.where(lane == width - 1, 0.0, pltpu.roll(value, width - 1, 1))
    return before, value, after


def net_layer_out(out, bias_i, b, u, dst, last):
    for k in range(8):
        block = jnp.concatenate(
            [jnp.maximum(out[k * 32 : k * 32 + 32, lanes(q)] + bias_i, 0.0) for q in range(4)], 1
        )
        if last:
            dst[u, (b * 8 + k) * 32 : (b * 8 + k) * 32 + 32, :] = block.astype(bf16)
            continue
        for t, piece in enumerate(taps_of(block)):
            piece = piece.astype(bf16)
            at = t * SEG + (k + 1) * 32
            dst[u, b, at : at + 32, :] = piece
            if b == 0 and k == 7:
                dst[u, 1, t * SEG : t * SEG + 32, :] = piece
            if b == 1 and k == 0:
                dst[u, 0, t * SEG + 288 : t * SEG + 320, :] = piece


def net_clear(ha, hb):
    for h in (ha, hb):
        for u in range(4):
            for t in range(3):
                zero = jnp.zeros((32, N), bf16)
                h[u, 0, t * SEG : t * SEG + 32, :] = zero
                h[u, 1, t * SEG + 288 : t * SEG + 320, :] = zero
            for b in range(2):
                h[u, b, DEPTH:1024, :] = jnp.zeros((1024 - DEPTH, N), bf16)


def net_run(nb, perm, w_first, w_mid, w_last, bias, ordered, ha, hb, hc, out_ref):
    ordered[...] = jnp.dot(perm[...], nb[...].reshape(B, N), preferred_element_type=f32)

    for u in range(4):
        zero = jnp.zeros((8, N), f32)
        parts = []
        for piece in taps_of(ordered[u * 32 : u * 32 + 32, :]):
            parts += [zero, piece, zero]
        stacked = jnp.concatenate(parts + [jnp.zeros((256 - 144, N), f32)], 0).astype(bf16)
        for b in range(2):
            out = jnp.dot(w_first[b * 256 : b * 256 + 256, :], stacked, preferred_element_type=f32)
            net_layer_out(out, bias[0], b, u, ha, False)
    for layer in range(2):
        src, dst = (ha, hb) if layer == 0 else (hb, hc)
        for u in range(4):
            for b in range(2):
                out = jnp.dot(w_mid[layer], src[u, b], preferred_element_type=f32)
                net_layer_out(out, bias[layer + 1], b, u, dst, layer == 1)
    for u in range(4):
        out = jnp.dot(w_last[...], hc[u], preferred_element_type=f32)
        before = taps_of(out[0:16, :])[0]
        after = taps_of(out[32:48, :])[2]
        out_ref[128 + u * 16 : 144 + u * 16, :] = before + out[16:32, :] + after


def main_kernel(
    obj,
    probe_hbm,
    amps_hbm,
    off,
    mats_hbm,
    slot_angle,
    conv_first,
    bias_first,
    conv_middle,
    bias_middle,
    conv_last,
    out,
    mats,
    pad,
    w_first,
    w_mid,
    w_last,
    bias,
    perm,
    ordered,
    ha,
    hb,
    hc,
    view,
    probe_in,
    amps_in,
    probe16,
    amp16,
    amp_send,
    amp_recv,
    off_own,
    off_send,
    off_recv,
    hot,
    tmp,
    pr,
    am,
    ya,
    yb,
    ff,
    x_obj,
    g_send,
    g_recv,
    g_own,
    sa,
    sb,
    ra,
    rb,
    total,
    as_send,
    nb,
    local_sem,
    x_sem,
    ag_recv,
    ring_send,
    sib_send,
    gs_sem,
    gr_sem,
    sa_sem,
    sb_sem,
    ra_sem,
    rb_sem,
    aa_send,
    aa_recv,
):
    pos = lax.axis_index("pos")
    ang = lax.axis_index("ang")
    c = lax.rem(pos, 2)
    s = lax.rem(pos // 2, 2)
    y = pos // 4
    me = 2 * s + c
    up = lax.rem(y + 1, 4)
    down = lax.rem(y + 3, 4)
    far = lax.rem(y + 2, 4)

    def at(yy, xx, cc):
        return yy * 4 + xx * 2 + cc

    dev_up = (ang, at(up, s, c))
    dev_down = (ang, at(down, s, c))
    dev_far = (ang, at(far, s, c))
    dev_x = (ang, at(y, 1 - s, c))
    dev_sib = (ang, at(y, s, 1 - c))
    step_size = learning / 16

    def put_obj(slot, value):
        for ri in range(2):
            out[pl.ds(pl.multiple_of(slot * 64 + ri * 32, 32), 32), :] = value[ri]

    def rc(src, dst, send, recv, dev):
        return pltpu.make_async_remote_copy(
            src_ref=src, dst_ref=dst, send_sem=send, recv_sem=recv, device_id=dev,
            device_id_type=MESH,
        )

    def arrived(dst, recv):
        rc(dst, dst, recv, recv, dev_x).wait_recv()

    def left_dev(src, send):
        rc(src, src, send, send, dev_x).wait_send()

    cp_probe = pltpu.make_async_copy(probe_hbm, probe_in, local_sem.at[0])
    cp_amps = pltpu.make_async_copy(amps_hbm, amps_in, local_sem.at[1])
    cp_mats = pltpu.make_async_copy(mats_hbm.at[0], mats.at[0], local_sem.at[2])
    cp_mats_mine = pltpu.make_async_copy(mats_hbm.at[me], mats.at[1], local_sem.at[3])
    cp_amps.start()
    cp_probe.start()
    cp_mats.start()
    cp_mats_mine.start()
    mat_l, mat_r = mats.at[0, 0], mats.at[0, 1]
    row_l, row_r = mats.at[1, 0], mats.at[1, 1]

    barrier = pltpu.get_barrier_semaphore()
    peers = [dev_up, dev_down, dev_far, dev_x, dev_sib]
    peers += [(ang, at(yy, 1 - s, c)) for yy in (up, down, far)]
    for dev in peers:
        pl.semaphore_signal(barrier, inc=1, device_id=dev, device_id_type=MESH)
    for d in range(1, 8):
        pl.semaphore_signal(
            barrier, inc=1, device_id=(lax.rem(ang + d, 8), pos), device_id_type=MESH
        )

    own = at(y, s, c)
    other = at(y, 1 - s, c)
    view[0, own] = obj[s].astype(bf16)
    x_obj[...] = obj[1 - s].astype(bf16)
    for i, (ref, slot) in enumerate(((off_own, s), (off_send, 1 - s))):
        for k in range(2):
            value = jnp.where(slot == 0, off[0, 0, k], off[1, 0, k])
            ref[k * 8 : k * 8 + 8, :] = jnp.full((8, 128), value, jnp.int32)

    pl.semaphore_wait(barrier, 15)

    rc(x_obj, view.at[0, own], x_sem.at[0], ag_recv.at[0, own], dev_x).start()
    rc(off_send, off_recv, x_sem.at[1], x_sem.at[2], dev_x).start()

    around = ((up, dev_up), (down, dev_down), (far, dev_far))

    def ag_start(k, xx):
        tile = at(y, xx, c)
        ref = view.at[k, tile]
        for d, (_, dev) in enumerate(around):
            rc(ref, ref, ring_send.at[k, xx, d], ag_recv.at[k, tile], dev).start()
        rc(ref, ref, sib_send.at[k, 3, xx], ag_recv.at[k, tile], dev_sib).start()

    def ag_relay(k, xx):
        for d, (yy, _) in enumerate(around):
            tile = at(yy, xx, c)
            ref = view.at[k, tile]
            arrived(ref, ag_recv.at[k, tile])
            rc(ref, ref, sib_send.at[k, d, xx], ag_recv.at[k, tile], dev_sib).start()

    def ag_rest(k, xx):
        for yy in range(4):
            tile = at(yy, xx, 1 - c)
            arrived(view.at[k, tile], ag_recv.at[k, tile])

    def ag_sent(k):
        for xx in range(2):
            tile = at(y, xx, c)
            for d in range(3):
                left_dev(view.at[k, tile], ring_send.at[k, xx, d])
            for d, yy in enumerate((up, down, far, y)):
                left_dev(view.at[k, at(yy, xx, c)], sib_send.at[k, d, xx])

    ag_start(0, s)
    cp_amps.wait()
    amp_send[...] = amps_in[1 - s, 0].astype(bf16)
    cp_amp_x = rc(amp_send, amp_recv, x_sem.at[3], x_sem.at[4], dev_x)
    cp_amp_x.start()
    amp16[...] = amps_in[s, 0].astype(bf16)
    arrived(view.at[0, other], ag_recv.at[0, other])
    ag_start(0, 1 - s)
    cp_probe.wait()
    probe16[...] = probe_in[...].astype(bf16)
    make_hot(off_own, 32 * me, hot.at[0])
    roll_plane(probe16.at[0], hot.at[0], tmp, pr.at[0, 0])
    roll_plane(probe16.at[1], hot.at[0], tmp, pr.at[0, 1])
    ag_relay(0, s)
    arrived(off_recv, x_sem.at[2])
    make_hot(off_recv, 32 * me, hot.at[1])
    roll_plane(probe16.at[0], hot.at[1], tmp, pr.at[1, 0])
    ag_relay(0, 1 - s)
    roll_plane(probe16.at[1], hot.at[1], tmp, pr.at[1, 1])
    cp_mats.wait()
    cp_mats_mine.wait()

    cols = (s, 1 - s)
    tiles = (me, 2 * s + 1 - c, 2 * (1 - s) + c, 2 * (1 - s) + 1 - c)

    def enter(k, *places):
        for place in places:
            stage1(view.at[k], pr, ya, tiles[place], place)
        for place in places:
            right(ya, mat_r, yb, bf16, place)

    def leave(g, place):
        right(yb, mat_l, ff, f32, place)
        stage3(ff, pr, g, place)

    def before_second(k):
        if k == 0:
            arrived(amp_recv, x_sem.at[4])
            roll_plane(amp_recv, hot.at[1], tmp, am.at[1])

    for k in range(2):
        if k == 1:
            ag_relay(k, s)
        enter(k, 0)
        if k == 1:
            ag_relay(k, 1 - s)
        ag_rest(k, s)
        enter(k, 1, 2)
        if k == 0:
            roll_plane(amp16, hot.at[0], tmp, am.at[0])
        ag_rest(k, 1 - s)
        enter(k, 3)
        middle(row_l, row_r, am, ya, yb, ff, functools.partial(before_second, k))
        order = (0, 1) if k == 0 else (1, 0)
        for o in order:
            leave(g_send.at[k, o], 2 * o + 1)
            rc(g_send.at[k, o], g_recv.at[k, o], gs_sem.at[k, o], gr_sem.at[k, o],
               dev_sib).start()

        def comb(yy, o):
            return g_own[o, yy] + g_recv[k, o, yy].astype(f32)

        if k == 0:
            for o in order:
                leave(g_own.at[o], 2 * o)
                arrived(g_recv.at[0, o], gr_sem.at[0, o])
                for d, (yy, dev) in ((2, around[2]), (0, around[0]), (1, around[1])):
                    sa[d, o] = comb(yy, o).astype(bf16)
                    rc(sa.at[d, o], ra.at[d, o], sa_sem.at[d, o], ra_sem.at[d, o], dev).start()
            ag_sent(0)
            net_weights(
                conv_first, bias_first, conv_middle, bias_middle, conv_last, pad, w_first, w_mid,
                w_last, bias,
            )
            for o in order:
                sum_x = comb(y, o)
                for d in range(3):
                    arrived(ra.at[d, o], ra_sem.at[d, o])
                    sum_x = sum_x + ra[d, o].astype(f32)
                total[o] = sum_x
                if o == 0:
                    view[1, own] = (obj[s] - step_size * sum_x).astype(bf16)
                else:
                    view[1, other] = (view[0, other].astype(f32) - step_size * sum_x).astype(bf16)
                ag_start(1, cols[o])
            make_perm(slot_angle, perm)
            net_clear(ha, hb)
            for d in range(3):
                for o in range(2):
                    left_dev(sa.at[d, o], sa_sem.at[d, o])
        else:
            for o in order:
                leave(g_own.at[o], 2 * o)
                arrived(g_recv.at[1, o], gr_sem.at[1, o])
                if o == 1:
                    sb[1, 3] = (comb(y, 1) + total[1]).astype(bf16)
                    rc(sb.at[1, 3], rb.at[1, 3], sb_sem.at[1, 3], rb_sem.at[1, 3], dev_x).start()
                for d, (yy, _) in ((2, around[2]), (0, around[0]), (1, around[1])):
                    sb[o, d] = comb(yy, o).astype(bf16)
                    rc(sb.at[o, d], rb.at[o, d], sb_sem.at[o, d], rb_sem.at[o, d],
                       (ang, at(yy, cols[o], c))).start()
            ag_sent(1)
            for d in range(4):
                arrived(rb.at[1, d], rb_sem.at[1, d])
            theirs = (
                rb[1, 0].astype(f32) + rb[1, 1].astype(f32) + rb[1, 2].astype(f32)
                + rb[1, 3].astype(f32)
            )
            put_obj(1 - s, obj[1 - s] - step_size * theirs)
            mine = comb(y, 0) + total[0]
            for d in range(3):
                arrived(rb.at[0, d], rb_sem.at[0, d])
                mine = mine + rb[0, d].astype(f32)
            put_obj(s, obj[s] - step_size * mine)
        for o in range(2):
            left_dev(g_send.at[k, o], gs_sem.at[k, o])

    for g in range(8):
        as_send[g] = jnp.concatenate(
            [out[q * 32 + g * 4 : q * 32 + g * 4 + 4, :] for q in range(4)], 0
        ).astype(bf16)

    def a2a(d):
        to = lax.rem(ang + d, 8)
        return rc(as_send.at[to], nb.at[ang], aa_send.at[d], aa_recv.at[ang], (to, pos))

    for d in range(1, 8):
        a2a(d).start()
    nb[ang] = as_send[ang]
    for d in range(1, 8):
        frm = lax.rem(ang + d, 8)
        arrived(nb.at[frm], aa_recv.at[frm])
    net_run(nb, perm, w_first, w_mid, w_last, bias, ordered, ha, hb, hc, out)
    for d in range(1, 8):
        a2a(d).wait_send()
    for o in range(2):
        for d in range(3 + o):
            left_dev(sb.at[o, d], sb_sem.at[o, d])
    left_dev(x_obj, x_sem.at[0])
    left_dev(off_send, x_sem.at[1])
    cp_amp_x.wait_send()


def split_kernel(both, obj_out, proj_out):
    obj_out[...] = both[0:128]
    proj_out[...] = both[128:192]


def split(both):
    vm = pl.BlockSpec(memory_space=pltpu.VMEM)
    return pl.pallas_call(
        split_kernel,
        out_shape=(
            jax.ShapeDtypeStruct((128, N), f32),
            jax.ShapeDtypeStruct((64, N), f32),
        ),
        in_specs=[vm],
        out_specs=(vm, vm),
    )(both)


def sweeps(
    object_init,
    probe_field,
    amplitudes,
    offsets,
    slot_angle,
    conv_first,
    bias_first,
    conv_middle,
    bias_middle,
    conv_last,
):
    mats = make_tables()
    vm = pl.BlockSpec(memory_space=pltpu.VMEM)
    hbm = pl.BlockSpec(memory_space=pltpu.HBM)
    smem = pl.BlockSpec(memory_space=pltpu.SMEM)
    tile = (2, 32, N)
    scratch = [
        pltpu.VMEM((2, 2, 4, 256, 256), bf16),
        pltpu.VMEM((9, 32, B), f32),
        pltpu.VMEM((N, 256), bf16),
        pltpu.VMEM((2, 256, 1024), bf16),
        pltpu.VMEM((48, N), bf16),
        pltpu.VMEM((3, 32, B), f32),
        pltpu.VMEM((B, B), bf16),
        pltpu.VMEM((B, N), f32),
        pltpu.VMEM((4, 2, 1024, N), bf16),
        pltpu.VMEM((4, 2, 1024, N), bf16),
        pltpu.VMEM((4, N, N), bf16),
        pltpu.VMEM((2, 16) + tile, bf16),
        pltpu.VMEM((2, N, N), f32),
        pltpu.VMEM((2, 1, N, N), f32),
        pltpu.VMEM((2, N, N), bf16),
        pltpu.VMEM((N, N), bf16),
        pltpu.VMEM((N, N), bf16),
        pltpu.VMEM((N, N), bf16),
        pltpu.VMEM((16, 128), jnp.int32),
        pltpu.VMEM((16, 128), jnp.int32),
        pltpu.VMEM((16, 128), jnp.int32),
        pltpu.VMEM((2, 2, N, N), bf16),
        pltpu.VMEM((N, N), bf16),
        pltpu.VMEM((2, 2, N, N), bf16),
        pltpu.VMEM((2, N, N), bf16),
        pltpu.VMEM((2, 2 * N, N), bf16),
        pltpu.VMEM((2, 2 * N, N), bf16),
        pltpu.VMEM((2, 2 * N, N), f32),
        pltpu.VMEM(tile, bf16),
        pltpu.VMEM((2, 2, 4) + tile, bf16),
        pltpu.VMEM((2, 2, 4) + tile, bf16),
        pltpu.VMEM((2, 4) + tile, f32),
        pltpu.VMEM((3, 2) + tile, bf16),
        pltpu.VMEM((2, 4) + tile, bf16),
        pltpu.VMEM((3, 2) + tile, bf16),
        pltpu.VMEM((2, 4) + tile, bf16),
        pltpu.VMEM((2,) + tile, f32),
        pltpu.VMEM((8, 16, N), bf16),
        pltpu.VMEM((8, 16, N), bf16),
        pltpu.SemaphoreType.DMA((4,)),
        pltpu.SemaphoreType.DMA((5,)),
        pltpu.SemaphoreType.DMA((2, 16)),
        pltpu.SemaphoreType.DMA((2, 2, 3)),
        pltpu.SemaphoreType.DMA((2, 4, 2)),
        pltpu.SemaphoreType.DMA((2, 2)),
        pltpu.SemaphoreType.DMA((2, 2)),
        pltpu.SemaphoreType.DMA((3, 2)),
        pltpu.SemaphoreType.DMA((2, 4)),
        pltpu.SemaphoreType.DMA((3, 2)),
        pltpu.SemaphoreType.DMA((2, 4)),
        pltpu.SemaphoreType.DMA((8,)),
        pltpu.SemaphoreType.DMA((8,)),
    ]
    return pl.pallas_call(
        main_kernel,
        out_shape=jax.ShapeDtypeStruct((192, N), f32),
        in_specs=[vm, hbm, hbm, smem, hbm, smem] + [vm] * 5,
        out_specs=vm,
        scratch_shapes=scratch,
        compiler_params=pltpu.CompilerParams(
            collective_id=0, has_side_effects=True, vmem_limit_bytes=60 << 20
        ),
        cost_estimate=pl.CostEstimate(
            flops=12_000_000_000, bytes_accessed=8_000_000, transcendentals=1_000_000
        ),
    )(
        object_init,
        probe_field,
        amplitudes,
        offsets,
        jnp.asarray(mats),
        slot_angle,
        conv_first.transpose(0, 1, 3, 2),
        bias_first.reshape(1, 32),
        conv_middle,
        bias_middle,
        conv_last,
    )


def on_device(
    object_init,
    probe_field,
    amplitudes,
    offsets,
    slot_angle,
    conv_first,
    bias_first,
    conv_middle,
    bias_middle,
    conv_last,
):
    both = sweeps(
        object_init,
        probe_field,
        amplitudes,
        offsets,
        slot_angle,
        conv_first,
        bias_first,
        conv_middle,
        bias_middle,
        conv_last,
    )
    obj_new, projections = split(both)
    return (obj_new.reshape(2, 2, 32, N), projections.reshape(1, 1, 4, 16, N))


def solution(mesh):
    return jax.shard_map(
        on_device,
        mesh=mesh,
        in_specs=(
            P("ang", None, "pos", None),
            P(),
            P("ang", "pos", None, None),
            P("ang", "pos", None),
            P(),
            P(),
            P(),
            P(),
            P(),
            P(),
        ),
        out_specs=(P("ang", None, "pos", None), P("pos", "ang", None, None, None)),
        check_vma=False,
    )
```

```python
import functools

import jax
import jax.numpy as jnp
import ml_dtypes
import numpy as np
from jax import lax
from jax.experimental import pallas as pl
from jax.experimental.pallas import tpu as pltpu
from jax.sharding import PartitionSpec as P

soften = 0.25
learning = 1.5
N = 512
B = 128
f32 = jnp.float32
bf16 = jnp.bfloat16
MESH = pl.DeviceIdType.MESH


def make_tables():
    f = np.arange(N)
    g = np.where(f < N // 2, f, f - N).astype(np.float64)
    lam = np.exp(-3j * np.pi * g * g / (4 * N))
    d = np.arange(B)[:, None] - np.arange(B)[None, :]
    blocks = []
    for m in range(4):
        fm = np.arange(m, N, 4)
        c = (lam[fm] * np.exp(2j * np.pi * fm * d[:, :, None] / N)).sum(-1) / N
        blocks.append(np.block([[c.real, -c.imag], [c.imag, c.real]]))
    left = np.stack(blocks)
    pair = np.stack([left, np.swapaxes(left, 1, 2)]).astype(ml_dtypes.bfloat16)
    orders = [np.arange(256) ^ (32 * k) for k in range(4)]
    return np.stack([pair[:, :, order][:, :, :, order] for order in orders])


def add(a, b):
    return (a[0] + b[0], a[1] + b[1])


def sub(a, b):
    return (a[0] - b[0], a[1] - b[1])


def add_i(a, b):
    return (a[0] - b[1], a[1] + b[0])


def sub_i(a, b):
    return (a[0] + b[1], a[1] - b[0])


def fold(x):
    t0, t1, t2, t3 = add(x[0], x[2]), sub(x[0], x[2]), add(x[1], x[3]), sub(x[1], x[3])
    return [add(t0, t2), sub_i(t1, t3), sub(t0, t2), add_i(t1, t3)]


def unfold(x):
    t0, t1, t2, t3 = add(x[0], x[2]), sub(x[0], x[2]), add(x[1], x[3]), sub(x[1], x[3])
    return [add(t0, t2), add_i(t1, t3), sub(t0, t2), sub_i(t1, t3)]


def fold2(e):
    rows = [fold(e[q]) for q in range(4)]
    cols = [fold([rows[q][m] for q in range(4)]) for m in range(4)]
    return [[cols[mc][mr] for mc in range(4)] for mr in range(4)]


def unfold2(e):
    cols = [unfold([e[q][m] for q in range(4)]) for m in range(4)]
    return [unfold([cols[m][q] for m in range(4)]) for q in range(4)]


def lanes(q):
    return slice(q * B, q * B + B)


def store_y(ya, y, row, n):
    for mr in range(4):
        for mc in range(4):
            for ri in range(2):
                at = (mr * 2 + ri) * B + row
                ya[at : at + n, lanes(mc)] = y[mr][mc][ri].astype(bf16)


def load_f(f, row, n):
    return [
        [
            tuple(
                f[(mr * 2 + ri) * B + row : (mr * 2 + ri) * B + row + n, lanes(mc)]
                for ri in range(2)
            )
            for mc in range(4)
        ]
        for mr in range(4)
    ]


ROWS = 16


def stage1(v, pr, ya, tile, place):
    n = ROWS
    for i in range(2):
        for part in range(0, 32, n):
            row = place * 32 + part
            e = []
            for q in range(4):
                line = []
                for c in range(4):
                    vr = v[q * 4 + tile, 0, part : part + n, lanes(c)].astype(f32)
                    vi = v[q * 4 + tile, 1, part : part + n, lanes(c)].astype(f32)
                    a = pr[i, 0, q * B + row : q * B + row + n, lanes(c)].astype(f32)
                    b = pr[i, 1, q * B + row : q * B + row + n, lanes(c)].astype(f32)
                    line.append((a * vr - b * vi, a * vi + b * vr))
                e.append(line)
            store_y(ya.at[i], fold2(e), row, n)


def right(ya, mats, out, dtype, place):
    rows = [(i, slice(m * B + place * 32, m * B + place * 32 + 32)) for i in range(2) for m in range(8)]
    for mc in range(4):
        lhs = jnp.concatenate(
            [
                jnp.concatenate([ya[i, at, lanes(mc)] for i, at in rows[p : p + 2]], 1)
                for p in range(0, 16, 2)
            ],
            0,
        )
        r = jnp.dot(lhs, mats[mc], preferred_element_type=f32)
        for p, (i, at) in enumerate(rows):
            out[i, at, lanes(mc)] = r[p // 2 * 32 : p // 2 * 32 + 32, lanes(p % 2)].astype(dtype)


def left_part(mats, yb, out, dtype, mr):
    at = slice(mr * 256, mr * 256 + 256)
    out[at, :] = jnp.dot(mats[mr], yb[at, :], preferred_element_type=f32).astype(dtype)


def stage2_part(f, am, ya, g):
    n = ROWS
    row = g * n
    w = unfold2(load_f(f, row, n))
    for q in range(4):
        for c in range(4):
            wr, wi = w[q][c]
            a = am[q * B + row : q * B + row + n, lanes(c)].astype(f32)
            s = 1.0 - a * lax.rsqrt(wr * wr + wi * wi + soften)
            w[q][c] = (wr * s, wi * s)
    store_y(ya, fold2(w), row, n)


def middle(mat_l, mat_r, am, ya, yb, ff, before_second):
    def lead(i, g):
        left_part(mat_l, yb.at[i], ff.at[i], f32, g)

    def back(i, g):
        left_part(mat_r, ya.at[i], yb.at[i], bf16, g)

    def misfit(i, g):
        for h in (2 * g, 2 * g + 1):
            stage2_part(ff.at[i], am.at[i], ya.at[i], h)

    for g in range(4):
        lead(0, g)
    for g in range(4):
        lead(1, g)
        misfit(0, g)
    before_second()
    for g in range(4):
        back(0, g)
        misfit(1, g)
    for g in range(4):
        back(1, g)


def stage3(f, pr, g, place):
    n = ROWS
    for part in range(0, 32, n):
        row = place * 32 + part
        tot = None
        for i in range(2):
            w = unfold2(load_f(f.at[i], row, n))
            new = []
            for q in range(4):
                for c in range(4):
                    a = pr[i, 0, q * B + row : q * B + row + n, lanes(c)].astype(f32)
                    b = pr[i, 1, q * B + row : q * B + row + n, lanes(c)].astype(f32)
                    br, bi = w[q][c]
                    new.append((a * br + b * bi, a * bi - b * br))
            tot = new if tot is None else [add(p, q) for p, q in zip(tot, new)]
        for q in range(4):
            for c in range(4):
                for ri in range(2):
                    g[q, ri, part : part + n, lanes(c)] = tot[q * 4 + c][ri].astype(g.dtype)


def one_hot(offset, order, transpose):
    a = lax.broadcasted_iota(jnp.int32, (N, N), 0)
    b = lax.broadcasted_iota(jnp.int32, (N, N), 1)
    if transpose:
        return jnp.where(a == ((b + offset) & (N - 1)), 1.0, 0.0).astype(bf16)
    return jnp.where(b == (((a ^ order) + offset) & (N - 1)), 1.0, 0.0).astype(bf16)


def make_hot(off, order, hot):
    hot[0] = one_hot(off[0:1, 0:1], order, False)
    hot[1] = one_hot(off[8:9, 0:1], order, True)


def roll_plane(src, hot, tmp, dst):
    for h in range(2):
        sl = slice(h * 256, h * 256 + 256)
        tmp[sl, :] = jnp.dot(hot[0, sl, :], src[...], preferred_element_type=f32).astype(bf16)
    for h in range(2):
        sl = slice(h * 256, h * 256 + 256)
        dst[sl, :] = jnp.dot(tmp[sl, :], hot[1], preferred_element_type=f32).astype(bf16)


SEG = 320
DEPTH = 3 * SEG


def net_weights(conv_first, bias_first, conv_middle, bias_middle, conv_last, pad, w_first, w_mid, w_last, bias):
    pad[...] = jnp.zeros_like(pad)
    for layer in range(2):
        for p in range(3):
            for t in range(3):
                pad[p * 3 + t, :, 0:32] = conv_middle[layer, p, t].astype(f32)
        turned = [
            [[pltpu.roll(pad[p * 3 + t], 32 * m, 1) if m else pad[p * 3 + t] for m in range(4)] for t in range(3)]
            for p in range(3)
        ]
        for k in range(8):
            blocks = [None] * 8
            for t in range(3):
                for p in range(3):
                    at = t * SEG + (k + p) * 32
                    piece = turned[p][t][at // 32 % 4]
                    held = blocks[at // B]
                    blocks[at // B] = piece if held is None else held + piece
            for j in range(8):
                value = jnp.zeros((32, B), f32) if blocks[j] is None else blocks[j]
                w_mid[layer, k * 32 : k * 32 + 32, lanes(j)] = value.astype(bf16)
    pad[...] = jnp.zeros_like(pad)
    square = pad.at[0:4]
    for p in range(3):
        for t in range(3):
            at = (p * 3 + t) * 8
            square[at // 32, at % 32 : at % 32 + 2, 0:32] = conv_first[p, t].astype(f32)
    flipped = jnp.transpose(pad[0:4].reshape(B, B))[0:32, :]
    group = lax.broadcasted_iota(jnp.int32, (32, B), 1) >> 3
    base = jnp.zeros((32, 256), f32)
    for p in range(3):
        for t in range(3):
            piece = jnp.where(group == p * 3 + t, flipped, 0.0)
            wide = jnp.concatenate([piece, jnp.zeros((32, B), f32)], 1)
            base = base + pltpu.roll(wide, (t * 48 + 6 + 2 * p - (p * 3 + t) * 8) % 256, 1)
    for k in range(16):
        w_first[k * 32 : k * 32 + 32, :] = (pltpu.roll(base, 2 * k, 1) if k else base).astype(bf16)
    pad[...] = jnp.zeros_like(pad)
    base = jnp.zeros((8, 640), f32)
    for p in range(3):
        pad[p, 0:3, 0:32] = conv_last[p].astype(f32)
        wide = jnp.concatenate([pad[p, 0:8, :], jnp.zeros((8, 512), f32)], 1)
        base = base + (pltpu.roll(wide, 32 * p, 1) if p else wide)
    row = lax.broadcasted_iota(jnp.int32, (16, N), 0)
    taps = [jnp.zeros((16, N), f32) for t in range(3)]
    for k in range(16):
        turned_k = (pltpu.roll(base, (32 * (k - 1)) % 640, 1) if k != 1 else base)[:, 0:N]
        for t in range(3):
            taps[t] = jnp.where(row == k, jnp.broadcast_to(turned_k[t : t + 1, :], (16, N)), taps[t])
    for t in range(3):
        w_last[t * 16 : t * 16 + 16, :] = taps[t].astype(bf16)
    eye = lax.broadcasted_iota(jnp.int32, (32, 32), 0) == lax.broadcasted_iota(jnp.int32, (32, 32), 1)
    for i in range(3):
        line = bias_first[0:1, :] if i == 0 else bias_middle[i - 1 : i, :]
        column = jnp.sum(jnp.where(eye, jnp.broadcast_to(line, (32, 32)), 0.0), axis=1, keepdims=True)
        bias[i] = jnp.broadcast_to(column, (32, B))


def make_perm(slot_angle, perm):
    r = lax.broadcasted_iota(jnp.int32, (B, B), 0)
    m = lax.broadcasted_iota(jnp.int32, (B, B), 1)
    angle = jnp.zeros((B, B), jnp.int32)
    for j in range(16):
        angle = jnp.where((m >> 3) == j, slot_angle[j], angle)
    hit = ((r >> 5) == (m & 3)) & ((r & 1) == ((m >> 2) & 1)) & (((r >> 1) & 15) == angle)
    perm[...] = jnp.where(hit, 1.0, 0.0).astype(bf16)


def taps_of(value):
    width = value.shape[1]
    lane = lax.broadcasted_iota(jnp.int32, value.shape, 1)
    before = jnp.where(lane == 0, 0.0, pltpu.roll(value, 1, 1))
    after = jnp.where(lane == width - 1, 0.0, pltpu.roll(value, width - 1, 1))
    return before, value, after


def net_layer_out(out, bias_i, b, u, dst, last):
    for k in range(8):
        block = jnp.concatenate(
            [jnp.maximum(out[k * 32 : k * 32 + 32, lanes(q)] + bias_i, 0.0) for q in range(4)], 1
        )
        if last:
            dst[u, (b * 8 + k) * 32 : (b * 8 + k) * 32 + 32, :] = block.astype(bf16)
            continue
        for t, piece in enumerate(taps_of(block)):
            piece = piece.astype(bf16)
            at = t * SEG + (k + 1) * 32
            dst[u, b, at : at + 32, :] = piece
            if b == 0 and k == 7:
                dst[u, 1, t * SEG : t * SEG + 32, :] = piece
            if b == 1 and k == 0:
                dst[u, 0, t * SEG + 288 : t * SEG + 320, :] = piece


def net_clear(ha, hb):
    for h in (ha, hb):
        for u in range(4):
            for t in range(3):
                zero = jnp.zeros((32, N), bf16)
                h[u, 0, t * SEG : t * SEG + 32, :] = zero
                h[u, 1, t * SEG + 288 : t * SEG + 320, :] = zero
            for b in range(2):
                h[u, b, DEPTH:1024, :] = jnp.zeros((1024 - DEPTH, N), bf16)


def net_run(nb, perm, w_first, w_mid, w_last, bias, ordered, ha, hb, hc, out_ref):
    ordered[...] = jnp.dot(perm[...], nb[...].reshape(B, N), preferred_element_type=f32)

    for u in range(4):
        zero = jnp.zeros((8, N), f32)
        parts = []
        for piece in taps_of(ordered[u * 32 : u * 32 + 32, :]):
            parts += [zero, piece, zero]
        stacked = jnp.concatenate(parts + [jnp.zeros((256 - 144, N), f32)], 0).astype(bf16)
        for b in range(2):
            out = jnp.dot(w_first[b * 256 : b * 256 + 256, :], stacked, preferred_element_type=f32)
            net_layer_out(out, bias[0], b, u, ha, False)
    for layer in range(2):
        src, dst = (ha, hb) if layer == 0 else (hb, hc)
        held = None
        for u in range(4):
            for b in range(2):
                out = jnp.dot(w_mid[layer], src[u, b], preferred_element_type=f32)
                if held is not None:
                    net_layer_out(held[0], bias[layer + 1], held[1], held[2], dst, layer == 1)
                held = (out, b, u)
        net_layer_out(held[0], bias[layer + 1], held[1], held[2], dst, layer == 1)
    for u in range(4):
        out = jnp.dot(w_last[...], hc[u], preferred_element_type=f32)
        before = taps_of(out[0:16, :])[0]
        after = taps_of(out[32:48, :])[2]
        out_ref[128 + u * 16 : 144 + u * 16, :] = before + out[16:32, :] + after


def main_kernel(
    obj,
    probe_hbm,
    amps_hbm,
    off,
    mats_hbm,
    slot_angle,
    conv_first,
    bias_first,
    conv_middle,
    bias_middle,
    conv_last,
    out,
    mats,
    pad,
    w_first,
    w_mid,
    w_last,
    bias,
    perm,
    ordered,
    ha,
    hb,
    hc,
    view,
    probe_in,
    amps_in,
    probe16,
    amp16,
    amp_send,
    amp_recv,
    off_own,
    off_send,
    off_recv,
    hot,
    tmp,
    pr,
    am,
    ya,
    yb,
    ff,
    x_obj,
    g_send,
    g_recv,
    g_own,
    sa,
    sb,
    ra,
    rb,
    total,
    as_send,
    nb,
    local_sem,
    x_sem,
    ag_recv,
    ring_send,
    sib_send,
    gs_sem,
    gr_sem,
    sa_sem,
    sb_sem,
    ra_sem,
    rb_sem,
    aa_send,
    aa_recv,
):
    pos = lax.axis_index("pos")
    ang = lax.axis_index("ang")
    c = lax.rem(pos, 2)
    s = lax.rem(pos // 2, 2)
    y = pos // 4
    me = 2 * s + c
    up = lax.rem(y + 1, 4)
    down = lax.rem(y + 3, 4)
    far = lax.rem(y + 2, 4)

    def at(yy, xx, cc):
        return yy * 4 + xx * 2 + cc

    dev_up = (ang, at(up, s, c))
    dev_down = (ang, at(down, s, c))
    dev_far = (ang, at(far, s, c))
    dev_x = (ang, at(y, 1 - s, c))
    dev_sib = (ang, at(y, s, 1 - c))
    step_size = learning / 16

    def put_obj(slot, value):
        for ri in range(2):
            out[pl.ds(pl.multiple_of(slot * 64 + ri * 32, 32), 32), :] = value[ri]

    def rc(src, dst, send, recv, dev):
        return pltpu.make_async_remote_copy(
            src_ref=src, dst_ref=dst, send_sem=send, recv_sem=recv, device_id=dev,
            device_id_type=MESH,
        )

    def arrived(dst, recv):
        rc(dst, dst, recv, recv, dev_x).wait_recv()

    def left_dev(src, send):
        rc(src, src, send, send, dev_x).wait_send()

    cp_probe = pltpu.make_async_copy(probe_hbm, probe_in, local_sem.at[0])
    cp_amps = pltpu.make_async_copy(amps_hbm, amps_in, local_sem.at[1])
    cp_mats = pltpu.make_async_copy(mats_hbm.at[0], mats.at[0], local_sem.at[2])
    cp_mats_mine = pltpu.make_async_copy(mats_hbm.at[me], mats.at[1], local_sem.at[3])
    cp_amps.start()
    cp_probe.start()
    cp_mats.start()
    cp_mats_mine.start()
    mat_l, mat_r = mats.at[0, 0], mats.at[0, 1]
    row_l, row_r = mats.at[1, 0], mats.at[1, 1]

    barrier = pltpu.get_barrier_semaphore()
    peers = [dev_up, dev_down, dev_far, dev_x, dev_sib]
    peers += [(ang, at(yy, 1 - s, c)) for yy in (up, down, far)]
    for dev in peers:
        pl.semaphore_signal(barrier, inc=1, device_id=dev, device_id_type=MESH)
    for d in range(1, 8):
        pl.semaphore_signal(
            barrier, inc=1, device_id=(lax.rem(ang + d, 8), pos), device_id_type=MESH
        )

    own = at(y, s, c)
    other = at(y, 1 - s, c)
    view[0, own] = obj[s].astype(bf16)
    x_obj[...] = obj[1 - s].astype(bf16)
    for i, (ref, slot) in enumerate(((off_own, s), (off_send, 1 - s))):
        for k in range(2):
            value = jnp.where(slot == 0, off[0, 0, k], off[1, 0, k])
            ref[k * 8 : k * 8 + 8, :] = jnp.full((8, 128), value, jnp.int32)

    pl.semaphore_wait(barrier, 15)

    rc(x_obj, view.at[0, own], x_sem.at[0], ag_recv.at[0, own], dev_x).start()
    rc(off_send, off_recv, x_sem.at[1], x_sem.at[2], dev_x).start()

    around = ((up, dev_up), (down, dev_down), (far, dev_far))

    def ag_start(k, xx):
        tile = at(y, xx, c)
        ref = view.at[k, tile]
        for d, (_, dev) in enumerate(around):
            rc(ref, ref, ring_send.at[k, xx, d], ag_recv.at[k, tile], dev).start()
        rc(ref, ref, sib_send.at[k, 3, xx], ag_recv.at[k, tile], dev_sib).start()

    def ag_relay(k, xx):
        for d, (yy, _) in enumerate(around):
            tile = at(yy, xx, c)
            ref = view.at[k, tile]
            arrived(ref, ag_recv.at[k, tile])
            rc(ref, ref, sib_send.at[k, d, xx], ag_recv.at[k, tile], dev_sib).start()

    def ag_rest(k, xx):
        for yy in range(4):
            tile = at(yy, xx, 1 - c)
            arrived(view.at[k, tile], ag_recv.at[k, tile])

    def ag_sent(k):
        for xx in range(2):
            tile = at(y, xx, c)
            for d in range(3):
                left_dev(view.at[k, tile], ring_send.at[k, xx, d])
            for d, yy in enumerate((up, down, far, y)):
                left_dev(view.at[k, at(yy, xx, c)], sib_send.at[k, d, xx])

    ag_start(0, s)
    cp_amps.wait()
    amp_send[...] = amps_in[1 - s, 0].astype(bf16)
    cp_amp_x = rc(amp_send, amp_recv, x_sem.at[3], x_sem.at[4], dev_x)
    cp_amp_x.start()
    amp16[...] = amps_in[s, 0].astype(bf16)
    arrived(view.at[0, other], ag_recv.at[0, other])
    ag_start(0, 1 - s)
    cp_probe.wait()
    probe16[...] = probe_in[...].astype(bf16)
    make_hot(off_own, 32 * me, hot.at[0])
    roll_plane(probe16.at[0], hot.at[0], tmp, pr.at[0, 0])
    roll_plane(probe16.at[1], hot.at[0], tmp, pr.at[0, 1])
    ag_relay(0, s)
    arrived(off_recv, x_sem.at[2])
    make_hot(off_recv, 32 * me, hot.at[1])
    roll_plane(probe16.at[0], hot.at[1], tmp, pr.at[1, 0])
    ag_relay(0, 1 - s)
    roll_plane(probe16.at[1], hot.at[1], tmp, pr.at[1, 1])
    cp_mats.wait()
    cp_mats_mine.wait()

    cols = (s, 1 - s)
    tiles = (me, 2 * s + 1 - c, 2 * (1 - s) + c, 2 * (1 - s) + 1 - c)

    def enter(k, *places):
        for place in places:
            stage1(view.at[k], pr, ya, tiles[place], place)
        for place in places:
            right(ya, mat_r, yb, bf16, place)

    def leave(g, places, at):
        if at == 0:
            right(yb, mat_l, ff, f32, places[0])
        if at < 3:
            right(yb, mat_l, ff, f32, places[at + 1])
        stage3(ff, pr, g, places[at])

    def before_second(k):
        if k == 0:
            arrived(amp_recv, x_sem.at[4])
            roll_plane(amp_recv, hot.at[1], tmp, am.at[1])

    for k in range(2):
        if k == 1:
            ag_relay(k, s)
        enter(k, 0)
        if k == 1:
            ag_relay(k, 1 - s)
        ag_rest(k, s)
        enter(k, 1, 2)
        if k == 0:
            roll_plane(amp16, hot.at[0], tmp, am.at[0])
        ag_rest(k, 1 - s)
        enter(k, 3)
        middle(row_l, row_r, am, ya, yb, ff, functools.partial(before_second, k))
        order = (0, 1) if k == 0 else (1, 0)
        places = [2 * o + 1 for o in order] + [2 * o for o in order]
        for o in order:
            leave(g_send.at[k, o], places, places.index(2 * o + 1))
            rc(g_send.at[k, o], g_recv.at[k, o], gs_sem.at[k, o], gr_sem.at[k, o],
               dev_sib).start()

        def comb(yy, o):
            return g_own[o, yy] + g_recv[k, o, yy].astype(f32)

        if k == 0:
            for o in order:
                leave(g_own.at[o], places, places.index(2 * o))
                arrived(g_recv.at[0, o], gr_sem.at[0, o])
                for d, (yy, dev) in ((2, around[2]), (0, around[0]), (1, around[1])):
                    sa[d, o] = comb(yy, o).astype(bf16)
                    rc(sa.at[d, o], ra.at[d, o], sa_sem.at[d, o], ra_sem.at[d, o], dev).start()
            ag_sent(0)
            net_weights(
                conv_first, bias_first, conv_middle, bias_middle, conv_last, pad, w_first, w_mid,
                w_last, bias,
            )
            for o in order:
                sum_x = comb(y, o)
                for d in range(3):
                    arrived(ra.at[d, o], ra_sem.at[d, o])
                    sum_x = sum_x + ra[d, o].astype(f32)
                total[o] = sum_x
                if o == 0:
                    view[1, own] = (obj[s] - step_size * sum_x).astype(bf16)
                else:
                    view[1, other] = (view[0, other].astype(f32) - step_size * sum_x).astype(bf16)
                ag_start(1, cols[o])
            make_perm(slot_angle, perm)
            net_clear(ha, hb)
            for d in range(3):
                for o in range(2):
                    left_dev(sa.at[d, o], sa_sem.at[d, o])
        else:
            for o in order:
                leave(g_own.at[o], places, places.index(2 * o))
                arrived(g_recv.at[1, o], gr_sem.at[1, o])
                if o == 1:
                    sb[1, 3] = (comb(y, 1) + total[1]).astype(bf16)
                    rc(sb.at[1, 3], rb.at[1, 3], sb_sem.at[1, 3], rb_sem.at[1, 3], dev_x).start()
                for d, (yy, _) in ((2, around[2]), (0, around[0]), (1, around[1])):
                    sb[o, d] = comb(yy, o).astype(bf16)
                    rc(sb.at[o, d], rb.at[o, d], sb_sem.at[o, d], rb_sem.at[o, d],
                       (ang, at(yy, cols[o], c))).start()
            ag_sent(1)
            for d in range(4):
                arrived(rb.at[1, d], rb_sem.at[1, d])
            theirs = (
                rb[1, 0].astype(f32) + rb[1, 1].astype(f32) + rb[1, 2].astype(f32)
                + rb[1, 3].astype(f32)
            )
            put_obj(1 - s, obj[1 - s] - step_size * theirs)
            mine = comb(y, 0) + total[0]
            for d in range(3):
                arrived(rb.at[0, d], rb_sem.at[0, d])
                mine = mine + rb[0, d].astype(f32)
            put_obj(s, obj[s] - step_size * mine)
        for o in range(2):
            left_dev(g_send.at[k, o], gs_sem.at[k, o])

    for g in range(8):
        as_send[g] = jnp.concatenate(
            [out[q * 32 + g * 4 : q * 32 + g * 4 + 4, :] for q in range(4)], 0
        ).astype(bf16)

    def a2a(d):
        to = lax.rem(ang + d, 8)
        return rc(as_send.at[to], nb.at[ang], aa_send.at[d], aa_recv.at[ang], (to, pos))

    for d in range(1, 8):
        a2a(d).start()
    nb[ang] = as_send[ang]
    for d in range(1, 8):
        frm = lax.rem(ang + d, 8)
        arrived(nb.at[frm], aa_recv.at[frm])
    net_run(nb, perm, w_first, w_mid, w_last, bias, ordered, ha, hb, hc, out)
    for d in range(1, 8):
        a2a(d).wait_send()
    for o in range(2):
        for d in range(3 + o):
            left_dev(sb.at[o, d], sb_sem.at[o, d])
    left_dev(x_obj, x_sem.at[0])
    left_dev(off_send, x_sem.at[1])
    cp_amp_x.wait_send()


def split_kernel(both, obj_out, proj_out):
    obj_out[...] = both[0:128]
    proj_out[...] = both[128:192]


def split(both):
    vm = pl.BlockSpec(memory_space=pltpu.VMEM)
    return pl.pallas_call(
        split_kernel,
        out_shape=(
            jax.ShapeDtypeStruct((128, N), f32),
            jax.ShapeDtypeStruct((64, N), f32),
        ),
        in_specs=[vm],
        out_specs=(vm, vm),
    )(both)


def sweeps(
    object_init,
    probe_field,
    amplitudes,
    offsets,
    slot_angle,
    conv_first,
    bias_first,
    conv_middle,
    bias_middle,
    conv_last,
):
    mats = make_tables()
    vm = pl.BlockSpec(memory_space=pltpu.VMEM)
    hbm = pl.BlockSpec(memory_space=pltpu.HBM)
    smem = pl.BlockSpec(memory_space=pltpu.SMEM)
    tile = (2, 32, N)
    scratch = [
        pltpu.VMEM((2, 2, 4, 256, 256), bf16),
        pltpu.VMEM((9, 32, B), f32),
        pltpu.VMEM((N, 256), bf16),
        pltpu.VMEM((2, 256, 1024), bf16),
        pltpu.VMEM((48, N), bf16),
        pltpu.VMEM((3, 32, B), f32),
        pltpu.VMEM((B, B), bf16),
        pltpu.VMEM((B, N), f32),
        pltpu.VMEM((4, 2, 1024, N), bf16),
        pltpu.VMEM((4, 2, 1024, N), bf16),
        pltpu.VMEM((4, N, N), bf16),
        pltpu.VMEM((2, 16) + tile, bf16),
        pltpu.VMEM((2, N, N), f32),
        pltpu.VMEM((2, 1, N, N), f32),
        pltpu.VMEM((2, N, N), bf16),
        pltpu.VMEM((N, N), bf16),
        pltpu.VMEM((N, N), bf16),
        pltpu.VMEM((N, N), bf16),
        pltpu.VMEM((16, 128), jnp.int32),
        pltpu.VMEM((16, 128), jnp.int32),
        pltpu.VMEM((16, 128), jnp.int32),
        pltpu.VMEM((2, 2, N, N), bf16),
        pltpu.VMEM((N, N), bf16),
        pltpu.VMEM((2, 2, N, N), bf16),
        pltpu.VMEM((2, N, N), bf16),
        pltpu.VMEM((2, 2 * N, N), bf16),
        pltpu.VMEM((2, 2 * N, N), bf16),
        pltpu.VMEM((2, 2 * N, N), f32),
        pltpu.VMEM(tile, bf16),
        pltpu.VMEM((2, 2, 4) + tile, bf16),
        pltpu.VMEM((2, 2, 4) + tile, bf16),
        pltpu.VMEM((2, 4) + tile, f32),
        pltpu.VMEM((3, 2) + tile, bf16),
        pltpu.VMEM((2, 4) + tile, bf16),
        pltpu.VMEM((3, 2) + tile, bf16),
        pltpu.VMEM((2, 4) + tile, bf16),
        pltpu.VMEM((2,) + tile, f32),
        pltpu.VMEM((8, 16, N), bf16),
        pltpu.VMEM((8, 16, N), bf16),
        pltpu.SemaphoreType.DMA((4,)),
        pltpu.SemaphoreType.DMA((5,)),
        pltpu.SemaphoreType.DMA((2, 16)),
        pltpu.SemaphoreType.DMA((2, 2, 3)),
        pltpu.SemaphoreType.DMA((2, 4, 2)),
        pltpu.SemaphoreType.DMA((2, 2)),
        pltpu.SemaphoreType.DMA((2, 2)),
        pltpu.SemaphoreType.DMA((3, 2)),
        pltpu.SemaphoreType.DMA((2, 4)),
        pltpu.SemaphoreType.DMA((3, 2)),
        pltpu.SemaphoreType.DMA((2, 4)),
        pltpu.SemaphoreType.DMA((8,)),
        pltpu.SemaphoreType.DMA((8,)),
    ]
    return pl.pallas_call(
        main_kernel,
        out_shape=jax.ShapeDtypeStruct((192, N), f32),
        in_specs=[vm, hbm, hbm, smem, hbm, smem] + [vm] * 5,
        out_specs=vm,
        scratch_shapes=scratch,
        compiler_params=pltpu.CompilerParams(
            collective_id=0, has_side_effects=True, vmem_limit_bytes=60 << 20
        ),
        cost_estimate=pl.CostEstimate(
            flops=12_000_000_000, bytes_accessed=8_000_000, transcendentals=1_000_000
        ),
    )(
        object_init,
        probe_field,
        amplitudes,
        offsets,
        jnp.asarray(mats),
        slot_angle,
        conv_first.transpose(0, 1, 3, 2),
        bias_first.reshape(1, 32),
        conv_middle,
        bias_middle,
        conv_last,
    )


def on_device(
    object_init,
    probe_field,
    amplitudes,
    offsets,
    slot_angle,
    conv_first,
    bias_first,
    conv_middle,
    bias_middle,
    conv_last,
):
    both = sweeps(
        object_init,
        probe_field,
        amplitudes,
        offsets,
        slot_angle,
        conv_first,
        bias_first,
        conv_middle,
        bias_middle,
        conv_last,
    )
    obj_new, projections = split(both)
    return (obj_new.reshape(2, 2, 32, N), projections.reshape(1, 1, 4, 16, N))


def solution(mesh):
    return jax.shard_map(
        on_device,
        mesh=mesh,
        in_specs=(
            P("ang", None, "pos", None),
            P(),
            P("ang", "pos", None, None),
            P("ang", "pos", None),
            P(),
            P(),
            P(),
            P(),
            P(),
            P(),
        ),
        out_specs=(P("ang", None, "pos", None), P("pos", "ang", None, None, None)),
        check_vma=False,
    )
```
